32 devices in a mesh: row: 16 (over z, x, core), col: 2 (over y).
Axes of the slice: x: 2, y: 2, z: 4, core: 2. Of those that a mesh axis runs over, the one named last changes fastest.
Arguments:
- image: bfloat16 [768, 512, 256], P('row', 'col'), may hold values from -6 to 6
- proj_in: bfloat16 [256, 512], replicated, may hold values from -0.375 to 0.375
- taps_wide: float32 [3, 512], replicated, may hold values from -3 to 3
- taps_tall: float32 [3, 512], replicated, may hold values from -3 to 3
- proj_out: bfloat16 [512, 256], replicated, may hold values from -0.25 to 0.25
- bias: float32 [256], replicated, may hold values from -3 to 3
Outputs:
- result: bfloat16 [768, 512, 256], P('row', 'col')
The draws below stay inside these ranges and needn't reach their ends.
All inputs are finite; a program needn't handle non-finite values.
Results may differ from the reference program's by a relative error of at most 0.0054.
Values may be sent and summed in bfloat16 or wider, within the bound.
No kernel may reach another device: no remote copies, remote signals or barrier semaphores. Data moves between devices by JAX's collectives and lax.ppermute only.
A program may use at most 192 MiB of HBM per device.

```python
import jax
import jax.numpy as jnp
from jax import lax

C = 256
R = 512
TH = 48
H = 768
W = 512
N_ROW = 16


def shard_levels(stream_key, dims, cuts, smallest, largest):
    gain = 1.0
    for axis_at, parts in cuts:
        heights = jax.random.uniform(jax.random.fold_in(jax.random.fold_in(stream_key, 6), axis_at), (parts,), jnp.float32, smallest / len(cuts), largest / len(cuts))
        gain = gain * jnp.repeat(jnp.exp(heights), dims[axis_at] // parts).reshape((-1,) + (1,) * (len(dims) - 1 - axis_at))
    return gain


def bell_draw(key, extent, width, bound, cuts=(), kind=jnp.bfloat16):
    entries = jax.random.normal(key, extent, jnp.float32) * width
    if len(cuts) > 0:
        entries = shard_levels(key, extent, cuts, -0.22, 0.18) * entries
    return jnp.clip(entries, min=-bound, max=bound).astype(kind)


def setup_inputs(seed: int = 0) -> dict:
    splits = jax.random.split(jax.random.key(seed), 7)
    image = bell_draw(splits[0], (H, W, C), 1.0, 6.0, ((0, 16), (1, 2)))
    proj_in = bell_draw(splits[1], (C, R), C ** -0.5, 0.375)
    taps_wide = bell_draw(splits[2], (3, R), 0.6, 3.0, (), jnp.float32)
    taps_tall = bell_draw(splits[3], (3, R), 0.6, 3.0, (), jnp.float32)
    proj_out = bell_draw(splits[4], (R, C), R ** -0.5, 0.25)
    bias = bell_draw(splits[5], (C,), 0.5, 3.0, (), jnp.float32)
    return {"image": image, "proj_in": proj_in, "taps_wide": taps_wide, "taps_tall": taps_tall, "proj_out": proj_out, "bias": bias}


def reference(image, proj_in, taps_wide, taps_tall, proj_out, bias):
    zero_row = jnp.zeros((1, W, C), jnp.bfloat16)
    padded_image = jnp.concatenate([zero_row, image, zero_row], axis=0)
    weight_in = proj_in.astype(jnp.float32)
    weight_out = proj_out.astype(jnp.float32)

    def one_block(index):
        rows = lax.dynamic_slice_in_dim(padded_image, (index * TH).astype(jnp.int32), TH + 2, 0)
        lifted = jnp.einsum("hwc,cr->hrw", rows.astype(jnp.float32), weight_in).astype(jnp.bfloat16)
        side = jnp.pad(lifted, ((0, 0), (0, 0), (1, 1)))
        widened = (taps_wide[0][:, None] * side[:, :, :-2] + taps_wide[1][:, None] * side[:, :, 1:-1]
                   + taps_wide[2][:, None] * side[:, :, 2:]).astype(jnp.bfloat16)
        heightened = (taps_tall[0][:, None] * widened[:-2] + taps_tall[1][:, None] * widened[1:-1]
                      + taps_tall[2][:, None] * widened[2:]).astype(jnp.bfloat16)
        mixed = jnp.einsum("hrw,rc->hwc", heightened.astype(jnp.float32), weight_out) + bias
        centre = rows[1:-1].astype(jnp.float32)
        return (centre + jax.nn.silu(mixed)).astype(jnp.bfloat16)

    blocks = lax.map(one_block, jnp.arange(N_ROW, dtype=jnp.int32))
    return blocks.reshape(H, W, C)
```

```python
import jax
import jax.numpy as jnp
from jax import lax
from jax.sharding import PartitionSpec as P

BF16 = jnp.bfloat16
F32 = jnp.float32


def shifted(x, axis, step):
    count = lax.axis_size(axis)
    if step > 0:
        return lax.ppermute(x, axis, [(i, i + 1) for i in range(count - 1)])
    return lax.ppermute(x, axis, [(i + 1, i) for i in range(count - 1)])


def column_halos(image):
    first, last = image[:, :1], image[:, -1:]
    if lax.axis_size("col") == 2:
        low = lax.axis_index("col") == 0
        got = lax.ppermute(jnp.where(low, last, first), "col", [(0, 1), (1, 0)])
        zero = jnp.zeros_like(got)
        return jnp.where(low, zero, got), jnp.where(low, got, zero)
    return shifted(last, "col", 1), shifted(first, "col", -1)


def dense_taps(proj_in, taps_wide, taps_tall, proj_out):
    c = proj_in.shape[0]
    scale = (taps_tall[:, None] * taps_wide[None]).reshape(9, 1, -1)
    scaled = (proj_in.astype(F32)[None] * scale).astype(BF16)
    taps = jnp.einsum("kcr,rd->kcd", scaled, proj_out, preferred_element_type=F32)
    return taps.astype(BF16).reshape(3, 3, c, c)


def on_device(image, proj_in, taps_wide, taps_tall, proj_out, bias):
    lh, rh = column_halos(image)
    taps = dense_taps(proj_in, taps_wide, taps_tall, proj_out)
    wide = jnp.concatenate([lh, image, rh], axis=1)
    top = shifted(wide[-1:], "row", 1)
    bot = shifted(wide[:1], "row", -1)
    padded = jnp.concatenate([top, wide, bot], axis=0)
    mixed = lax.conv_general_dilated(
        padded[None], taps, (1, 1), "VALID",
        dimension_numbers=("NHWC", "HWIO", "NHWC"), preferred_element_type=F32)[0]
    return (image.astype(F32) + jax.nn.silu(mixed + bias)).astype(BF16)


def solution(mesh):
    in_specs = (P("row", "col", None), P(), P(), P(), P(), P())
    out_specs = P("row", "col", None)
    return jax.shard_map(
        on_device, mesh=mesh, in_specs=in_specs, out_specs=out_specs, check_vma=False
    )
```

```python
import jax
import jax.numpy as jnp
from jax import lax
from jax.experimental import pallas as pl
from jax.experimental.pallas import tpu as pltpu
from jax.sharding import PartitionSpec as P

BF16 = jnp.bfloat16
F32 = jnp.float32
MIB = 1 << 20
ROWS = 4


def conv_kernel(before, here, after, top, bot, u_ref, lh_ref, rh_ref, bias_ref, out_ref, shifts):
    i = pl.program_id(0)
    n, w, c = here.shape
    ring = lax.broadcasted_iota(jnp.int32, (w, c), 0)
    first = jnp.where(i == 0, top[0:w, :], before[0])
    last = jnp.where(i == pl.num_programs(0) - 1, bot[0:w, :], after[0])
    rows = [first] + [here[r] for r in range(n)] + [last]
    for r, x in enumerate(rows):
        at = i * n + r
        x32 = x.astype(F32)
        lead, tail = lh_ref[pl.ds(at, 1), :], rh_ref[pl.ds(at, 1), :]
        shifts[r, 0] = jnp.where(ring == 0, lead, pltpu.roll(x32, 1, 0)).astype(BF16)
        shifts[r, 1] = x
        shifts[r, 2] = jnp.where(ring == w - 1, tail, pltpu.roll(x32, w - 1, 0)).astype(BF16)
    lhs = [
        jnp.concatenate([shifts[r + k // 3, k % 3] for k in range(9)], axis=1) for r in range(n)
    ]
    y = jnp.dot(jnp.concatenate(lhs, axis=0), u_ref[...], preferred_element_type=F32)
    bias = bias_ref[...] * 0.5
    for r in range(n):
        half = y[r * w : (r + 1) * w] + bias
        out_ref[r] = (here[r].astype(F32) + (half + half * jnp.tanh(half))).astype(BF16)


def shifted(x, axis, step):
    count = lax.axis_size(axis)
    if step > 0:
        return lax.ppermute(x, axis, [(i, i + 1) for i in range(count - 1)])
    return lax.ppermute(x, axis, [(i + 1, i) for i in range(count - 1)])


def column_halos(image):
    first, last = image[:, 0, :], image[:, -1, :]
    if lax.axis_size("col") == 2:
        low = lax.axis_index("col") == 0
        got = lax.ppermute(jnp.where(low, last, first), "col", [(0, 1), (1, 0)])
        zero = jnp.zeros_like(got)
        return jnp.where(low, zero, got), jnp.where(low, got, zero)
    return shifted(last, "col", 1), shifted(first, "col", -1)


def dense_taps(proj_in, taps_wide, taps_tall, proj_out):
    c = proj_in.shape[0]
    scale = (taps_tall[:, None] * taps_wide[None] * 0.5).reshape(9, 1, -1)
    scaled = (proj_in.astype(F32)[None] * scale).astype(BF16)
    taps = jnp.einsum("kcr,rd->kcd", scaled, proj_out, preferred_element_type=F32)
    return taps.astype(BF16).reshape(9 * c, c)


def on_device(image, proj_in, taps_wide, taps_tall, proj_out, bias):
    th, w, c = image.shape
    lh, rh = column_halos(image)
    u = dense_taps(proj_in, taps_wide, taps_tall, proj_out)

    def extended(at):
        pad = jnp.zeros((14, c), BF16)
        return jnp.concatenate([image[at], lh[at][None], rh[at][None], pad], axis=0)

    top = shifted(extended(-1), "row", 1)
    bot = shifted(extended(0), "row", -1)

    def column(x, at):
        pad = jnp.zeros((6, c), BF16)
        return jnp.concatenate([top[at][None], x, bot[at][None], pad], axis=0).astype(F32)

    def whole(x):
        return pl.BlockSpec(x.shape, lambda i: (0,) * x.ndim)

    small = (top, bot, u, column(lh, w), column(rh, w + 1), bias.reshape(1, c))
    block = pl.BlockSpec((ROWS, w, c), lambda i: (i, 0, 0))
    return pl.pallas_call(
        conv_kernel,
        grid=(th // ROWS,),
        out_shape=jax.ShapeDtypeStruct(image.shape, BF16),
        in_specs=[
            pl.BlockSpec((1, w, c), lambda i: (jnp.maximum(i * ROWS - 1, 0), 0, 0)),
            block,
            pl.BlockSpec((1, w, c), lambda i: (jnp.minimum(i * ROWS + ROWS, th - 1), 0, 0)),
            *[whole(x) for x in small],
        ],
        out_specs=block,
        scratch_shapes=[pltpu.VMEM((ROWS + 2, 3, w, c), BF16)],
        compiler_params=pltpu.CompilerParams(vmem_limit_bytes=48 * MIB),
        name="conv",
    )(image, image, image, *small)


def solution(mesh):
    in_specs = (P("row", "col", None), P(), P(), P(), P(), P())
    out_specs = P("row", "col", None)
    return jax.shard_map(
        on_device, mesh=mesh, in_specs=in_specs, out_specs=out_specs, check_vma=False
    )
```

```python
import functools

import jax
import jax.numpy as jnp
from jax import lax
from jax.experimental import pallas as pl
from jax.experimental.pallas import tpu as pltpu
from jax.sharding import PartitionSpec as P

BF16 = jnp.bfloat16
F32 = jnp.float32
MIB = 1 << 20
ROWS = 4


def side_columns(x, lead, tail):
    w = x.shape[0]
    at = lax.broadcasted_iota(jnp.int32, x.shape, 0)
    x32 = x.astype(F32)
    left = jnp.where(at == 0, lead, pltpu.roll(x32, 1, 0))
    right = jnp.where(at == w - 1, tail, pltpu.roll(x32, w - 1, 0))
    return left.astype(BF16), right.astype(BF16)


def convolve(rows, u_ref):
    pairs = range((len(rows) - 2) // 2)

    def term(k, a, b, add):
        parts = []
        for p in pairs:
            sums = [x() + y() if add else x() - y() for x, y in zip(rows[2 * p + a], rows[2 * p + b])]
            parts.append(jnp.concatenate(sums, axis=1))
        lhs = parts[0] if len(parts) == 1 else jnp.concatenate(parts, axis=0)
        return jnp.dot(lhs, u_ref[k], preferred_element_type=F32)

    m1 = term(1, 1, 2, True)
    m2 = term(2, 2, 1, False)
    m0 = term(0, 0, 2, False)
    m3 = term(3, 1, 3, False)
    return m0 + (m1 + m2), (m1 - m2) - m3


def finish(centre, half):
    return (centre.astype(F32) + (half + half * jnp.tanh(half))).astype(BF16)


def store_rows(here, ya, yb, bias_ref, out_ref):
    n, w, _ = here.shape
    bias = bias_ref[...] * 0.5
    for r in range(n):
        y = yb if r % 2 else ya
        part = y[(r // 2) * w : (r // 2 + 1) * w]
        out_ref[r] = finish(here[r], part + bias)


def inner_kernel(before, here, after, u_ref, lh_ref, rh_ref, bias_ref, out_ref, sides):
    i = pl.program_id(0)
    n = here.shape[0]
    base = (i + 1) * n
    centres = [functools.partial(before.__getitem__, 0)]
    centres += [functools.partial(here.__getitem__, r) for r in range(n)]
    centres += [functools.partial(after.__getitem__, 0)]

    def shift(r):
        at = base - 1 + r
        left, right = side_columns(centres[r](), lh_ref[pl.ds(at, 1), :], rh_ref[pl.ds(at, 1), :])
        sides[r, 0] = left
        sides[r, 1] = right

    @pl.when(i == 0)
    def _():
        shift(0)
        shift(1)

    @pl.when(i > 0)
    def _():
        sides[0:2] = sides[n : n + 2]

    for r in range(2, n + 2):
        shift(r)
    rows = [
        (functools.partial(sides.__getitem__, (r, 0)), centres[r],
         functools.partial(sides.__getitem__, (r, 1)))
        for r in range(n + 2)
    ]
    ya, yb = convolve(rows, u_ref)
    store_rows(here, ya, yb, bias_ref, out_ref)


def edge_kernel(here, second, top, bot, u_ref, lh_ref, rh_ref, bias_ref, out_ref, shifts):
    i = pl.program_id(0)
    n, w, _ = here.shape
    height = lh_ref.shape[0] - 8
    rows = [jnp.where(i == 0, top[0:w, :], second[0])]
    rows += [here[r] for r in range(n)]
    rows += [jnp.where(i == 0, second[0], bot[0:w, :])]
    base = i * (height - n)
    for r, x in enumerate(rows):
        lead, tail = lh_ref[pl.ds(base + r, 1), :], rh_ref[pl.ds(base + r, 1), :]
        shifts[r, 0], shifts[r, 2] = side_columns(x, lead, tail)
        shifts[r, 1] = x
    getters = [
        tuple(functools.partial(shifts.__getitem__, (r, k)) for k in range(3)) for r in range(n + 2)
    ]
    ya, yb = convolve(getters, u_ref)
    store_rows(here, ya, yb, bias_ref, out_ref)


def shifted(x, axis, step):
    count = lax.axis_size(axis)
    if step > 0:
        return lax.ppermute(x, axis, [(i, i + 1) for i in range(count - 1)])
    return lax.ppermute(x, axis, [(i + 1, i) for i in range(count - 1)])


def column_halos(image):
    first, last = image[:, 0, :], image[:, -1, :]
    if lax.axis_size("col") == 2:
        low = lax.axis_index("col") == 0
        got = lax.ppermute(jnp.where(low, last, first), "col", [(0, 1), (1, 0)])
        zero = jnp.zeros_like(got)
        return jnp.where(low, zero, got), jnp.where(low, got, zero)
    return shifted(last, "col", 1), shifted(first, "col", -1)


def transformed_taps(proj_in, taps_wide, taps_tall, proj_out):
    c = proj_in.shape[0]
    t0, t1, t2 = taps_tall
    mid = 0.5 * (t0 + t2)
    tall = jnp.stack([t0, mid + 0.5 * t1, mid - 0.5 * t1, t2])
    scale = (tall[:, None] * taps_wide[None] * 0.5).reshape(12, 1, -1)
    scaled = (proj_in.astype(F32)[None] * scale).astype(BF16)
    u = jnp.einsum("kcr,rd->kcd", scaled, proj_out, preferred_element_type=F32)
    return u.astype(BF16).reshape(4, 3 * c, c)


def on_device(image, proj_in, taps_wide, taps_tall, proj_out, bias):
    th, w, c = image.shape
    n = ROWS
    lh, rh = column_halos(image)
    u = transformed_taps(proj_in, taps_wide, taps_tall, proj_out)

    def extended(at):
        pad = jnp.zeros((14, c), BF16)
        return jnp.concatenate([image[at], lh[at][None], rh[at][None], pad], axis=0)

    top = shifted(extended(-1), "row", 1)
    bot = shifted(extended(0), "row", -1)

    def column(x, at):
        pad = jnp.zeros((6, c), BF16)
        return jnp.concatenate([top[at][None], x, bot[at][None], pad], axis=0).astype(F32)

    def whole(x):
        return pl.BlockSpec(x.shape, lambda i: (0,) * x.ndim)

    def one_row(index):
        return pl.BlockSpec((1, w, c), lambda i: (index(i), 0, 0))

    def cost(rows):
        return pl.CostEstimate(
            flops=rows * 12 * w * c * c, bytes_accessed=4 * rows * w * c, transcendentals=rows * w * c)

    params = pltpu.CompilerParams(vmem_limit_bytes=48 * MIB)
    bias2 = bias.reshape(1, c)
    small = (u, lh.astype(F32), rh.astype(F32), bias2)
    inner = pl.pallas_call(
        inner_kernel,
        grid=(th // n - 2,),
        out_shape=jax.ShapeDtypeStruct(image.shape, BF16),
        in_specs=[
            one_row(lambda i: (i + 1) * n - 1),
            pl.BlockSpec((n, w, c), lambda i: (i + 1, 0, 0)),
            one_row(lambda i: (i + 2) * n),
            *[whole(x) for x in small],
        ],
        out_specs=pl.BlockSpec((n, w, c), lambda i: (i + 1, 0, 0)),
        scratch_shapes=[pltpu.VMEM((n + 2, 2, w, c), BF16)],
        compiler_params=params,
        cost_estimate=cost(th - 2 * n),
        name="inner",
    )(image, image, image, *small)

    small = (top, bot, u, column(lh, w), column(rh, w + 1), bias2)
    edges = pl.pallas_call(
        edge_kernel,
        grid=(2,),
        out_shape=jax.ShapeDtypeStruct((2 * n, w, c), BF16),
        in_specs=[
            pl.BlockSpec((n, w, c), lambda i: (i * (th // n - 1), 0, 0)),
            one_row(lambda i: n + i * (th - 2 * n - 1)),
            *[whole(x) for x in small],
        ],
        out_specs=pl.BlockSpec((n, w, c), lambda i: (i, 0, 0)),
        scratch_shapes=[pltpu.VMEM((n + 2, 3, w, c), BF16)],
        compiler_params=params,
        cost_estimate=cost(2 * n),
        name="edges",
    )(image, image, *small)
    out = lax.dynamic_update_slice(inner, edges[:n], (0, 0, 0))
    return lax.dynamic_update_slice(out, edges[n:], (th - n, 0, 0))


def solution(mesh):
    in_specs = (P("row", "col", None), P(), P(), P(), P(), P())
    out_specs = P("row", "col", None)
    return jax.shard_map(
        on_device, mesh=mesh, in_specs=in_specs, out_specs=out_specs, check_vma=False
    )
```

```python
import jax
import jax.numpy as jnp
from jax import lax
from jax.experimental import pallas as pl
from jax.experimental.pallas import tpu as pltpu
from jax.sharding import PartitionSpec as P

BF16 = jnp.bfloat16
F32 = jnp.float32
MIB = 1 << 20
ROWS = 8


def side_columns(x, lead, tail):
    w = x.shape[0]
    at = lax.broadcasted_iota(jnp.int32, x.shape, 0)
    x32 = x.astype(F32)
    left = jnp.where(at == 0, lead, pltpu.roll(x32, 1, 0))
    right = jnp.where(at == w - 1, tail, pltpu.roll(x32, w - 1, 0))
    return left.astype(BF16), right.astype(BF16)


def conv_kernel(before, here, after, top, bot, u_ref, lh_ref, rh_ref, bias_ref, out_ref,
                ends, sides):
    i = pl.program_id(0)
    n, w, _ = here.shape
    bias = bias_ref[...] * 0.5

    def centre(r):
        return here[r - 1] if 0 < r <= n else ends[r // n]

    def shift(r):
        at = i * n + r
        lead, tail = lh_ref[pl.ds(at, 1), :], rh_ref[pl.ds(at, 1), :]
        sides[r, 0], sides[r, 1] = side_columns(centre(r), lead, tail)

    def row(r):
        return sides[r, 0], centre(r), sides[r, 1]

    def product(k, a, b, add):
        sums = [x + y if add else x - y for x, y in zip(row(a), row(b))]
        return jnp.dot(jnp.concatenate(sums, axis=1), u_ref[k], preferred_element_type=F32)

    def finish(r, half):
        x = here[r].astype(F32)
        out_ref[r] = (x + (half + half * jnp.tanh(half))).astype(BF16)

    ends[0] = jnp.where(i == 0, top[0:w, :], before[0])
    ends[1] = jnp.where(i == pl.num_programs(0) - 1, bot[0:w, :], after[0])
    shift(0)
    shift(1)
    for r in range(0, n, 2):
        shift(r + 2)
        shift(r + 3)
        m1 = product(1, r + 1, r + 2, True)
        m2 = product(2, r + 2, r + 1, False)
        m0 = product(0, r, r + 2, False)
        m3 = product(3, r + 1, r + 3, False)
        finish(r, m0 + (m1 + m2) + bias)
        finish(r + 1, (m1 - m2) - m3 + bias)


def shifted(x, axis, step):
    count = lax.axis_size(axis)
    if step > 0:
        return lax.ppermute(x, axis, [(i, i + 1) for i in range(count - 1)])
    return lax.ppermute(x, axis, [(i + 1, i) for i in range(count - 1)])


def column_halos(image):
    first, last = image[:, 0, :], image[:, -1, :]
    if lax.axis_size("col") == 2:
        low = lax.axis_index("col") == 0
        got = lax.ppermute(jnp.where(low, last, first), "col", [(0, 1), (1, 0)])
        zero = jnp.zeros_like(got)
        return jnp.where(low, zero, got), jnp.where(low, got, zero)
    return shifted(last, "col", 1), shifted(first, "col", -1)


def transformed_taps(proj_in, taps_wide, taps_tall, proj_out):
    c = proj_in.shape[0]
    t0, t1, t2 = taps_tall
    mid = 0.5 * (t0 + t2)
    tall = jnp.stack([t0, mid + 0.5 * t1, mid - 0.5 * t1, t2])
    scale = (tall[:, None] * taps_wide[None] * 0.5).reshape(12, 1, -1)
    scaled = (proj_in.astype(F32)[None] * scale).astype(BF16)
    u = jnp.einsum("kcr,rd->kcd", scaled, proj_out, preferred_element_type=F32)
    return u.astype(BF16).reshape(4, 3 * c, c)


def on_device(image, proj_in, taps_wide, taps_tall, proj_out, bias):
    th, w, c = image.shape
    n = ROWS
    lh, rh = column_halos(image)
    u = transformed_taps(proj_in, taps_wide, taps_tall, proj_out)

    def extended(at):
        pad = jnp.zeros((14, c), BF16)
        return jnp.concatenate([image[at], lh[at][None], rh[at][None], pad], axis=0)

    top = shifted(extended(-1), "row", 1)
    bot = shifted(extended(0), "row", -1)

    def column(x, at):
        pad = jnp.zeros((6, c), BF16)
        return jnp.concatenate([top[at][None], x, bot[at][None], pad], axis=0).astype(F32)

    def whole(x):
        return pl.BlockSpec(x.shape, lambda i: (0,) * x.ndim)

    def one_row(index):
        return pl.BlockSpec((1, w, c), lambda i: (index(i), 0, 0))

    small = (top, bot, u, column(lh, w), column(rh, w + 1), bias.reshape(1, c))
    block = pl.BlockSpec((n, w, c), lambda i: (i, 0, 0))
    return pl.pallas_call(
        conv_kernel,
        grid=(th // n,),
        out_shape=jax.ShapeDtypeStruct(image.shape, BF16),
        in_specs=[
            one_row(lambda i: jnp.maximum(i * n - 1, 0)),
            block,
            one_row(lambda i: jnp.minimum(i * n + n, th - 1)),
            *[whole(x) for x in small],
        ],
        out_specs=block,
        scratch_shapes=[pltpu.VMEM((2, w, c), BF16), pltpu.VMEM((n + 2, 2, w, c), BF16)],
        compiler_params=pltpu.CompilerParams(vmem_limit_bytes=48 * MIB),
        name="conv",
    )(image, image, image, *small)


def solution(mesh):
    in_specs = (P("row", "col", None), P(), P(), P(), P(), P())
    out_specs = P("row", "col", None)
    return jax.shard_map(
        on_device, mesh=mesh, in_specs=in_specs, out_specs=out_specs, check_vma=False
    )
```

```python
import functools

import jax
import jax.numpy as jnp
from jax import lax
from jax.experimental import pallas as pl
from jax.experimental.pallas import tpu as pltpu
from jax.sharding import PartitionSpec as P

BF16 = jnp.bfloat16
F32 = jnp.float32
MIB = 1 << 20
ROWS = 4


def side_columns(x, lead, tail):
    w = x.shape[0]
    at = lax.broadcasted_iota(jnp.int32, x.shape, 0)
    x32 = x.astype(F32)
    left = jnp.where(at == 0, lead, pltpu.roll(x32, 1, 0))
    right = jnp.where(at == w - 1, tail, pltpu.roll(x32, w - 1, 0))
    return left.astype(BF16), right.astype(BF16)


def convolve(rows, u_ref):
    pairs = range((len(rows) - 2) // 2)

    def term(k, a, b, add):
        parts = []
        for p in pairs:
            sums = [x() + y() if add else x() - y() for x, y in zip(rows[2 * p + a], rows[2 * p + b])]
            parts.append(jnp.concatenate(sums, axis=1))
        lhs = parts[0] if len(parts) == 1 else jnp.concatenate(parts, axis=0)
        return jnp.dot(lhs, u_ref[k], preferred_element_type=F32)

    m1 = term(1, 1, 2, True)
    m2 = term(2, 2, 1, False)
    m0 = term(0, 0, 2, False)
    m3 = term(3, 1, 3, False)
    return m0 + (m1 + m2), (m1 - m2) - m3


def finish(centre, half):
    return (centre.astype(F32) + (half + half * jnp.tanh(half))).astype(BF16)


def store_rows(here, ya, yb, bias_ref, out_ref):
    n, w, _ = here.shape
    bias = bias_ref[...] * 0.5
    for r in range(n):
        y = yb if r % 2 else ya
        part = y[(r // 2) * w : (r // 2 + 1) * w]
        out_ref[r] = finish(here[r], part + bias)


def inner_kernel(before, here, after, u_ref, lh_ref, rh_ref, bias_ref, out_ref, sides):
    i = pl.program_id(0)
    n = here.shape[0]
    base = (i + 1) * n
    centres = [functools.partial(before.__getitem__, 0)]
    centres += [functools.partial(here.__getitem__, r) for r in range(n)]
    centres += [functools.partial(after.__getitem__, 0)]

    def shift(r):
        at = base - 1 + r
        left, right = side_columns(centres[r](), lh_ref[pl.ds(at, 1), :], rh_ref[pl.ds(at, 1), :])
        sides[r, 0] = left
        sides[r, 1] = right

    @pl.when(i == 0)
    def _():
        shift(0)
        shift(1)

    @pl.when(i > 0)
    def _():
        sides[0:2] = sides[n : n + 2]

    for r in range(2, n + 2):
        shift(r)
    rows = [
        (functools.partial(sides.__getitem__, (r, 0)), centres[r],
         functools.partial(sides.__getitem__, (r, 1)))
        for r in range(n + 2)
    ]
    ya, yb = convolve(rows, u_ref)
    store_rows(here, ya, yb, bias_ref, out_ref)


def edge_kernel(here, second, top, bot, u_ref, lh_ref, rh_ref, bias_ref, out_ref, shifts):
    i = pl.program_id(0)
    n, w, _ = here.shape
    height = lh_ref.shape[0] - 8
    rows = [jnp.where(i == 0, top[0:w, :], second[0])]
    rows += [here[r] for r in range(n)]
    rows += [jnp.where(i == 0, second[0], bot[0:w, :])]
    base = i * (height - n)
    for r, x in enumerate(rows):
        lead, tail = lh_ref[pl.ds(base + r, 1), :], rh_ref[pl.ds(base + r, 1), :]
        shifts[r, 0], shifts[r, 2] = side_columns(x, lead, tail)
        shifts[r, 1] = x
    getters = [
        tuple(functools.partial(shifts.__getitem__, (r, k)) for k in range(3)) for r in range(n + 2)
    ]
    ya, yb = convolve(getters, u_ref)
    store_rows(here, ya, yb, bias_ref, out_ref)


def shifted(x, axis, step):
    count = lax.axis_size(axis)
    if step > 0:
        return lax.ppermute(x, axis, [(i, i + 1) for i in range(count - 1)])
    return lax.ppermute(x, axis, [(i + 1, i) for i in range(count - 1)])


def row_halos(first, last):
    count, me = lax.axis_size("row"), lax.axis_index("row")
    if count % 2:
        return shifted(last, "row", 1), shifted(first, "row", -1)
    even = me % 2 == 0
    below = [[i, i + 1] for i in range(0, count, 2)]
    above = [[i, (i + 1) % count] for i in range(1, count, 2)]
    ga = lax.all_gather(jnp.where(even, last, first), "row", axis_index_groups=below)
    gb = lax.all_gather(jnp.where(even, first, last), "row", axis_index_groups=above)
    top = jnp.where(even, gb[0], ga[0])
    bot = jnp.where(even, ga[1], gb[1])
    top = jnp.where(me == 0, jnp.zeros_like(top), top)
    bot = jnp.where(me == count - 1, jnp.zeros_like(bot), bot)
    return top, bot


def column_halos(image):
    first, last = image[:, 0, :], image[:, -1, :]
    if lax.axis_size("col") == 2:
        low = lax.axis_index("col") == 0
        got = lax.ppermute(jnp.where(low, last, first), "col", [(0, 1), (1, 0)])
        zero = jnp.zeros_like(got)
        return jnp.where(low, zero, got), jnp.where(low, got, zero)
    return shifted(last, "col", 1), shifted(first, "col", -1)


def transformed_taps(proj_in, taps_wide, taps_tall, proj_out):
    c = proj_in.shape[0]
    t0, t1, t2 = taps_tall
    mid = 0.5 * (t0 + t2)
    tall = jnp.stack([t0, mid + 0.5 * t1, mid - 0.5 * t1, t2])
    scale = (tall[:, None] * taps_wide[None] * 0.5).reshape(12, 1, -1)
    scaled = (proj_in.astype(F32)[None] * scale).astype(BF16)
    u = jnp.einsum("kcr,rd->kcd", scaled, proj_out, preferred_element_type=F32)
    return u.astype(BF16).reshape(4, 3 * c, c)


def on_device(image, proj_in, taps_wide, taps_tall, proj_out, bias):
    th, w, c = image.shape
    n = ROWS
    lh, rh = column_halos(image)
    u = transformed_taps(proj_in, taps_wide, taps_tall, proj_out)

    def extended(at):
        pad = jnp.zeros((14, c), BF16)
        return jnp.concatenate([image[at], lh[at][None], rh[at][None], pad], axis=0)

    top, bot = row_halos(extended(0), extended(-1))

    def column(x, at):
        pad = jnp.zeros((6, c), BF16)
        return jnp.concatenate([top[at][None], x, bot[at][None], pad], axis=0).astype(F32)

    def whole(x):
        return pl.BlockSpec(x.shape, lambda i: (0,) * x.ndim)

    def one_row(index):
        return pl.BlockSpec((1, w, c), lambda i: (index(i), 0, 0))

    def cost(rows):
        return pl.CostEstimate(
            flops=rows * 12 * w * c * c, bytes_accessed=4 * rows * w * c, transcendentals=rows * w * c)

    params = pltpu.CompilerParams(vmem_limit_bytes=48 * MIB)
    bias2 = bias.reshape(1, c)
    small = (u, lh.astype(F32), rh.astype(F32), bias2)
    inner = pl.pallas_call(
        inner_kernel,
        grid=(th // n - 2,),
        out_shape=jax.ShapeDtypeStruct(image.shape, BF16),
        in_specs=[
            one_row(lambda i: (i + 1) * n - 1),
            pl.BlockSpec((n, w, c), lambda i: (i + 1, 0, 0)),
            one_row(lambda i: (i + 2) * n),
            *[whole(x) for x in small],
        ],
        out_specs=pl.BlockSpec((n, w, c), lambda i: (i + 1, 0, 0)),
        scratch_shapes=[pltpu.VMEM((n + 2, 2, w, c), BF16)],
        compiler_params=params,
        cost_estimate=cost(th - 2 * n),
        name="inner",
    )(image, image, image, *small)

    small = (top, bot, u, column(lh, w), column(rh, w + 1), bias2)
    edges = pl.pallas_call(
        edge_kernel,
        grid=(2,),
        out_shape=jax.ShapeDtypeStruct((2 * n, w, c), BF16),
        in_specs=[
            pl.BlockSpec((n, w, c), lambda i: (i * (th // n - 1), 0, 0)),
            one_row(lambda i: n + i * (th - 2 * n - 1)),
            *[whole(x) for x in small],
        ],
        out_specs=pl.BlockSpec((n, w, c), lambda i: (i, 0, 0)),
        scratch_shapes=[pltpu.VMEM((n + 2, 3, w, c), BF16)],
        compiler_params=params,
        cost_estimate=cost(2 * n),
        name="edges",
    )(image, image, *small)
    out = lax.dynamic_update_slice(inner, edges[:n], (0, 0, 0))
    return lax.dynamic_update_slice(out, edges[n:], (th - n, 0, 0))


def solution(mesh):
    in_specs = (P("row", "col", None), P(), P(), P(), P(), P())
    out_specs = P("row", "col", None)
    return jax.shard_map(
        on_device, mesh=mesh, in_specs=in_specs, out_specs=out_specs, check_vma=False
    )
```

```python
import jax
import jax.numpy as jnp
from jax import lax
from jax.experimental import pallas as pl
from jax.experimental.pallas import tpu as pltpu
from jax.sharding import PartitionSpec as P

BF16 = jnp.bfloat16
F32 = jnp.float32
MIB = 1 << 20
ROWS = 8


def side_columns(x, lead, tail):
    w = x.shape[0]
    at = lax.broadcasted_iota(jnp.int32, x.shape, 0)
    x32 = x.astype(F32)
    left = jnp.where(at == 0, lead, pltpu.roll(x32, 1, 0))
    right = jnp.where(at == w - 1, tail, pltpu.roll(x32, w - 1, 0))
    return left.astype(BF16), right.astype(BF16)


def conv_kernel(before, here, after, top, bot, u_ref, lh_ref, rh_ref, bias_ref, out_ref,
                ends, sides, halves):
    i = pl.program_id(0)
    n, w, _ = here.shape
    bias = bias_ref[...] * 0.5

    def centre(r):
        return here[r - 1] if 0 < r <= n else ends[r // n]

    def shift(r):
        at = i * n + r
        lead, tail = lh_ref[pl.ds(at, 1), :], rh_ref[pl.ds(at, 1), :]
        sides[r, 0], sides[r, 1] = side_columns(centre(r), lead, tail)

    def row(r):
        return sides[r, 0], centre(r), sides[r, 1]

    def product(k, a, b, add):
        sums = [x + y if add else x - y for x, y in zip(row(a), row(b))]
        return jnp.dot(jnp.concatenate(sums, axis=1), u_ref[k], preferred_element_type=F32)

    def finish(r):
        if r >= 0:
            half = halves[r // 2 % 2, r % 2]
            x = here[r].astype(F32)
            out_ref[r] = (x + (half + half * jnp.tanh(half))).astype(BF16)

    ends[1] = jnp.where(i == pl.num_programs(0) - 1, bot[0:w, :], after[0])

    @pl.when(i == 0)
    def _():
        ends[0] = top[0:w, :]
        shift(0)
        shift(1)

    @pl.when(i > 0)
    def _():
        ends[0] = before[0]
        sides[0:2] = sides[n : n + 2]

    shift(2)
    shift(3)
    for r in range(0, n, 2):
        m1 = product(1, r + 1, r + 2, True)
        finish(r - 2)
        m2 = product(2, r + 2, r + 1, False)
        finish(r - 1)
        m0 = product(0, r, r + 2, False)
        if r + 2 < n:
            shift(r + 4)
        m3 = product(3, r + 1, r + 3, False)
        if r + 2 < n:
            shift(r + 5)
        halves[r // 2 % 2, 0] = m0 + (m1 + m2) + bias
        halves[r // 2 % 2, 1] = (m1 - m2) - m3 + bias
    finish(n - 2)
    finish(n - 1)


def shifted(x, axis, step):
    count = lax.axis_size(axis)
    if step > 0:
        return lax.ppermute(x, axis, [(i, i + 1) for i in range(count - 1)])
    return lax.ppermute(x, axis, [(i + 1, i) for i in range(count - 1)])


def column_halos(image):
    first, last = image[:, 0, :], image[:, -1, :]
    if lax.axis_size("col") == 2:
        low = lax.axis_index("col") == 0
        got = lax.ppermute(jnp.where(low, last, first), "col", [(0, 1), (1, 0)])
        zero = jnp.zeros_like(got)
        return jnp.where(low, zero, got), jnp.where(low, got, zero)
    return shifted(last, "col", 1), shifted(first, "col", -1)


def transformed_taps(proj_in, taps_wide, taps_tall, proj_out):
    c = proj_in.shape[0]
    t0, t1, t2 = taps_tall
    mid = 0.5 * (t0 + t2)
    tall = jnp.stack([t0, mid + 0.5 * t1, mid - 0.5 * t1, t2])
    scale = (tall[:, None] * taps_wide[None] * 0.5).reshape(12, 1, -1)
    scaled = (proj_in.astype(F32)[None] * scale).astype(BF16)
    u = jnp.einsum("kcr,rd->kcd", scaled, proj_out, preferred_element_type=F32)
    return u.astype(BF16).reshape(4, 3 * c, c)


def on_device(image, proj_in, taps_wide, taps_tall, proj_out, bias):
    th, w, c = image.shape
    n = ROWS
    lh, rh = column_halos(image)
    u = transformed_taps(proj_in, taps_wide, taps_tall, proj_out)

    def extended(at):
        pad = jnp.zeros((14, c), BF16)
        return jnp.concatenate([image[at], lh[at][None], rh[at][None], pad], axis=0)

    top = shifted(extended(-1), "row", 1)
    bot = shifted(extended(0), "row", -1)

    def column(x, at):
        pad = jnp.zeros((6, c), BF16)
        return jnp.concatenate([top[at][None], x, bot[at][None], pad], axis=0).astype(F32)

    def whole(x):
        return pl.BlockSpec(x.shape, lambda i: (0,) * x.ndim)

    def one_row(index):
        return pl.BlockSpec((1, w, c), lambda i: (index(i), 0, 0))

    small = (top, bot, u, column(lh, w), column(rh, w + 1), bias.reshape(1, c))
    block = pl.BlockSpec((n, w, c), lambda i: (i, 0, 0))
    return pl.pallas_call(
        conv_kernel,
        grid=(th // n,),
        out_shape=jax.ShapeDtypeStruct(image.shape, BF16),
        in_specs=[
            one_row(lambda i: jnp.maximum(i * n - 1, 0)),
            block,
            one_row(lambda i: jnp.minimum(i * n + n, th - 1)),
            *[whole(x) for x in small],
        ],
        out_specs=block,
        scratch_shapes=[pltpu.VMEM((2, w, c), BF16), pltpu.VMEM((n + 2, 2, w, c), BF16),
                        pltpu.VMEM((2, 2, w, c), F32)],
        compiler_params=pltpu.CompilerParams(vmem_limit_bytes=48 * MIB),
        name="conv",
    )(image, image, image, *small)


def solution(mesh):
    in_specs = (P("row", "col", None), P(), P(), P(), P(), P())
    out_specs = P("row", "col", None)
    return jax.shard_map(
        on_device, mesh=mesh, in_specs=in_specs, out_specs=out_specs, check_vma=False
    )
```

```python
import functools

import jax
import jax.numpy as jnp
from jax import lax
from jax.experimental import pallas as pl
from jax.experimental.pallas import tpu as pltpu
from jax.sharding import PartitionSpec as P

BF16 = jnp.bfloat16
F32 = jnp.float32
MIB = 1 << 20
ROWS = 16
PART = 8


def side_columns(x, lead, tail):
    w = x.shape[0]
    at = lax.broadcasted_iota(jnp.int32, x.shape, 0)
    x32 = x.astype(F32)
    left = jnp.where(at == 0, lead, pltpu.roll(x32, 1, 0))
    right = jnp.where(at == w - 1, tail, pltpu.roll(x32, w - 1, 0))
    return left.astype(BF16), right.astype(BF16)


def conv_kernel(before, here, after, top, bot, u_ref, lh_ref, rh_ref, bias_ref, out_ref,
                ends, sides, halves):
    i = pl.program_id(0)
    n, w, _ = here.shape
    bias = bias_ref[...] * 0.5

    def centre(r):
        return here[r - 1] if 0 < r <= n else ends[r // n]

    def shift(r):
        at = i * n + r
        lead, tail = lh_ref[pl.ds(at, 1), :], rh_ref[pl.ds(at, 1), :]
        sides[r, 0], sides[r, 1] = side_columns(centre(r), lead, tail)

    def row(r):
        return sides[r, 0], centre(r), sides[r, 1]

    def product(k, start, a, b, add):
        lhs = []
        for r in range(start, start + PART, 2):
            sums = [x + y if add else x - y for x, y in zip(row(r + a), row(r + b))]
            lhs.append(jnp.concatenate(sums, axis=1))
        return jnp.dot(jnp.concatenate(lhs, axis=0), u_ref[k], preferred_element_type=F32)

    def finish(r):
        half = halves[r]
        x = here[r].astype(F32)
        out_ref[r] = (x + (half + half * jnp.tanh(half))).astype(BF16)

    ends[1] = jnp.where(i == pl.num_programs(0) - 1, bot[0:w, :], after[0])

    @pl.when(i == 0)
    def _():
        ends[0] = top[0:w, :]
        shift(0)
        shift(1)

    @pl.when(i > 0)
    def _():
        ends[0] = before[0]
        sides[0:2] = sides[n : n + 2]

    for r in range(PART):
        shift(r + 2)
    for start in range(0, n, PART):
        later = [functools.partial(finish, r) for r in range(start - PART, start) if r >= 0]
        later += [functools.partial(shift, start + PART + 2 + r) for r in range(PART) if start + PART < n]
        later = [later[q::4] for q in range(4)]
        m1 = product(1, start, 1, 2, True)
        for call in later[0]:
            call()
        m2 = product(2, start, 2, 1, False)
        for call in later[1]:
            call()
        m0 = product(0, start, 0, 2, False)
        for call in later[2]:
            call()
        m3 = product(3, start, 1, 3, False)
        for call in later[3]:
            call()
        ya = m0 + (m1 + m2) + bias
        yb = (m1 - m2) - m3 + bias
        for r in range(0, PART, 2):
            at = slice(r // 2 * w, (r // 2 + 1) * w)
            halves[start + r] = ya[at]
            halves[start + r + 1] = yb[at]
    for r in range(n - PART, n):
        finish(r)


def shifted(x, axis, step):
    count = lax.axis_size(axis)
    if step > 0:
        return lax.ppermute(x, axis, [(i, i + 1) for i in range(count - 1)])
    return lax.ppermute(x, axis, [(i + 1, i) for i in range(count - 1)])


def column_halos(image):
    first, last = image[:, 0, :], image[:, -1, :]
    if lax.axis_size("col") == 2:
        low = lax.axis_index("col") == 0
        got = lax.ppermute(jnp.where(low, last, first), "col", [(0, 1), (1, 0)])
        zero = jnp.zeros_like(got)
        return jnp.where(low, zero, got), jnp.where(low, got, zero)
    return shifted(last, "col", 1), shifted(first, "col", -1)


def transformed_taps(proj_in, taps_wide, taps_tall, proj_out):
    c = proj_in.shape[0]
    t0, t1, t2 = taps_tall
    mid = 0.5 * (t0 + t2)
    tall = jnp.stack([t0, mid + 0.5 * t1, mid - 0.5 * t1, t2])
    scale = (tall[:, None] * taps_wide[None] * 0.5).reshape(12, 1, -1)
    scaled = (proj_in.astype(F32)[None] * scale).astype(BF16)
    u = jnp.einsum("kcr,rd->kcd", scaled, proj_out, preferred_element_type=F32)
    return u.astype(BF16).reshape(4, 3 * c, c)


def on_device(image, proj_in, taps_wide, taps_tall, proj_out, bias):
    th, w, c = image.shape
    n = ROWS
    lh, rh = column_halos(image)
    u = transformed_taps(proj_in, taps_wide, taps_tall, proj_out)

    def extended(at):
        pad = jnp.zeros((14, c), BF16)
        return jnp.concatenate([image[at], lh[at][None], rh[at][None], pad], axis=0)

    top = shifted(extended(-1), "row", 1)
    bot = shifted(extended(0), "row", -1)

    def column(x, at):
        pad = jnp.zeros((6, c), BF16)
        return jnp.concatenate([top[at][None], x, bot[at][None], pad], axis=0).astype(F32)

    def whole(x):
        return pl.BlockSpec(x.shape, lambda i: (0,) * x.ndim)

    def one_row(index):
        return pl.BlockSpec((1, w, c), lambda i: (index(i), 0, 0))

    small = (top, bot, u, column(lh, w), column(rh, w + 1), bias.reshape(1, c))
    block = pl.BlockSpec((n, w, c), lambda i: (i, 0, 0))
    return pl.pallas_call(
        conv_kernel,
        grid=(th // n,),
        out_shape=jax.ShapeDtypeStruct(image.shape, BF16),
        in_specs=[
            one_row(lambda i: jnp.maximum(i * n - 1, 0)),
            block,
            one_row(lambda i: jnp.minimum(i * n + n, th - 1)),
            *[whole(x) for x in small],
        ],
        out_specs=block,
        scratch_shapes=[pltpu.VMEM((2, w, c), BF16), pltpu.VMEM((n + 2, 2, w, c), BF16),
                        pltpu.VMEM((n, w, c), F32)],
        compiler_params=pltpu.CompilerParams(vmem_limit_bytes=48 * MIB),
        name="conv",
    )(image, image, image, *small)


def solution(mesh):
    in_specs = (P("row", "col", None), P(), P(), P(), P(), P())
    out_specs = P("row", "col", None)
    return jax.shard_map(
        on_device, mesh=mesh, in_specs=in_specs, out_specs=out_specs, check_vma=False
    )
```

```python
import jax
import jax.numpy as jnp
from jax import lax
from jax.experimental import pallas as pl
from jax.experimental.pallas import tpu as pltpu
from jax.sharding import PartitionSpec as P

BF16 = jnp.bfloat16
F32 = jnp.float32
MIB = 1 << 20
ROWS = 8


def side_columns(x, lead, tail):
    w = x.shape[0]
    at = lax.broadcasted_iota(jnp.int32, x.shape, 0)
    x32 = x.astype(F32)
    left = jnp.where(at == 0, lead, pltpu.roll(x32, 1, 0))
    right = jnp.where(at == w - 1, tail, pltpu.roll(x32, w - 1, 0))
    return left.astype(BF16), right.astype(BF16)


def conv_kernel(before, here, after, top, bot, u_ref, lh_ref, rh_ref, bias_ref, out_ref,
                ends, sides):
    i = pl.program_id(0)
    n, w, _ = here.shape
    bias = bias_ref[...] * 0.5

    def centre(r):
        return here[r - 1] if 0 < r <= n else ends[r // n]

    def shift(r):
        at = i * n + r
        lead, tail = lh_ref[pl.ds(at, 1), :], rh_ref[pl.ds(at, 1), :]
        sides[r, 0], sides[r, 1] = side_columns(centre(r), lead, tail)

    def row(r):
        return sides[r, 0], centre(r), sides[r, 1]

    def product(k, a, b, add):
        sums = [x + y if add else x - y for x, y in zip(row(a), row(b))]
        return jnp.dot(jnp.concatenate(sums, axis=1), u_ref[k], preferred_element_type=F32)

    def finish(r, half):
        x = here[r].astype(F32)
        out_ref[r] = (x + (half + half * jnp.tanh(half))).astype(BF16)

    ends[0] = jnp.where(i == 0, top[...], before[0])
    ends[1] = jnp.where(i == pl.num_programs(0) - 1, bot[...], after[0])
    shift(0)
    shift(1)
    for r in range(0, n, 2):
        shift(r + 2)
        shift(r + 3)
        m1 = product(1, r + 1, r + 2, True)
        m2 = product(2, r + 2, r + 1, False)
        m0 = product(0, r, r + 2, False)
        m3 = product(3, r + 1, r + 3, False)
        finish(r, m0 + (m1 + m2) + bias)
        finish(r + 1, (m1 - m2) - m3 + bias)


def ends_kernel(first, last, left, right, rows_ref, cols_ref):
    rows_ref[0] = first[0]
    rows_ref[1] = last[0]
    for r in range(left.shape[0]):
        cols_ref[0, r : r + 1, :] = left[r].astype(F32)[:1]
        cols_ref[1, r : r + 1, :] = right[r].astype(F32)[-1:]


def weights_kernel(pin_ref, tw_ref, tt_ref, po_ref, u_ref, scaled):
    pin = pin_ref[...].astype(F32)
    c = pin.shape[0]
    t0, t1, t2 = tt_ref[0:1, :], tt_ref[1:2, :], tt_ref[2:3, :]
    mid = 0.5 * (t0 + t2)
    for k, tall in enumerate((t0, mid + 0.5 * t1, mid - 0.5 * t1, t2)):
        for j in range(3):
            scaled[3 * k + j] = (pin * (tall * tw_ref[j : j + 1, :] * 0.5)).astype(BF16)
    for k in range(4):
        for j in range(3):
            u = jnp.dot(scaled[3 * k + j], po_ref[...], preferred_element_type=F32)
            u_ref[k, j * c : (j + 1) * c, :] = u.astype(BF16)


def shifted(x, axis, step):
    count = lax.axis_size(axis)
    if step > 0:
        return lax.ppermute(x, axis, [(i, i + 1) for i in range(count - 1)])
    return lax.ppermute(x, axis, [(i + 1, i) for i in range(count - 1)])


def row_halos(first, last):
    count = lax.axis_size("row")
    if count % 2:
        return shifted(last, "row", 1), shifted(first, "row", -1)
    even = lax.axis_index("row") % 2 == 0

    def swap(x, start):
        pairs = [(i, i + 1) for i in range(start, count - 1, 2)]
        return lax.ppermute(x, "row", pairs + [(b, a) for a, b in pairs])

    got = swap(jnp.where(even, last, first), 0)
    far = swap(jnp.where(even, first, last), 1)
    return jnp.where(even, far, got), jnp.where(even, got, far)


def column_halos(first, last):
    if lax.axis_size("col") == 2:
        low = lax.axis_index("col") == 0
        got = lax.ppermute(jnp.where(low, last, first), "col", [(0, 1), (1, 0)])
        zero = jnp.zeros_like(got)
        return jnp.where(low, zero, got), jnp.where(low, got, zero)
    return shifted(last, "col", 1), shifted(first, "col", -1)


def on_device(image, proj_in, taps_wide, taps_tall, proj_out, bias):
    th, w, c = image.shape
    n = ROWS

    def whole(x):
        return pl.BlockSpec(x.shape, lambda i: (0,) * len(x.shape))

    def one_row(index):
        return pl.BlockSpec((1, w, c), lambda i: (index(i), 0, 0))

    def some_columns(at):
        return pl.BlockSpec((th, 16, c), lambda i: (0, at, 0))

    params = pltpu.CompilerParams(vmem_limit_bytes=48 * MIB)
    ends = jax.ShapeDtypeStruct((2, w, c), BF16), jax.ShapeDtypeStruct((2, th, c), F32)
    rows, cols = pl.pallas_call(
        ends_kernel,
        grid=(1,),
        out_shape=ends,
        in_specs=[one_row(lambda i: 0), one_row(lambda i: th - 1),
                  some_columns(0), some_columns(w // 16 - 1)],
        out_specs=tuple(whole(x) for x in ends),
        compiler_params=params,
        name="ends",
    )(image, image, image, image)
    top, bot = row_halos(rows[0], rows[1])

    args = (proj_in, taps_wide, taps_tall, proj_out)
    weights = jax.ShapeDtypeStruct((4, 3 * c, c), BF16)
    u = pl.pallas_call(
        weights_kernel,
        grid=(1,),
        out_shape=weights,
        in_specs=[whole(x) for x in args],
        out_specs=whole(weights),
        scratch_shapes=[pltpu.VMEM((12,) + proj_in.shape, BF16)],
        compiler_params=params,
        cost_estimate=pl.CostEstimate(
            flops=24 * c * c * proj_in.shape[1], bytes_accessed=3 * MIB, transcendentals=0),
        name="weights",
    )(*args)

    def column(k, at):
        pad = jnp.zeros((14, c), BF16)
        return jnp.concatenate(
            [top[at][None], cols[k].astype(BF16), bot[at][None], pad], axis=0)

    lh, rh = column_halos(column(0, 0), column(1, w - 1))
    small = (top, bot, u, lh.astype(F32), rh.astype(F32), bias.reshape(1, c))
    block = pl.BlockSpec((n, w, c), lambda i: (i, 0, 0))
    return pl.pallas_call(
        conv_kernel,
        grid=(th // n,),
        out_shape=jax.ShapeDtypeStruct(image.shape, BF16),
        in_specs=[
            one_row(lambda i: jnp.maximum(i * n - 1, 0)),
            block,
            one_row(lambda i: jnp.minimum(i * n + n, th - 1)),
            *[whole(x) for x in small],
        ],
        out_specs=block,
        scratch_shapes=[pltpu.VMEM((2, w, c), BF16), pltpu.VMEM((n + 2, 2, w, c), BF16)],
        compiler_params=params,
        name="conv",
    )(image, image, image, *small)


def solution(mesh):
    in_specs = (P("row", "col", None), P(), P(), P(), P(), P())
    out_specs = P("row", "col", None)
    return jax.shard_map(
        on_device, mesh=mesh, in_specs=in_specs, out_specs=out_specs, check_vma=False
    )
```

```python
import jax
import jax.numpy as jnp
from jax import lax
from jax.experimental import pallas as pl
from jax.experimental.pallas import tpu as pltpu
from jax.sharding import PartitionSpec as P

BF16 = jnp.bfloat16
F32 = jnp.float32
MIB = 1 << 20
ROWS = 4


def side_columns(x, lead, tail):
    w = x.shape[0]
    at = lax.broadcasted_iota(jnp.int32, x.shape, 0)
    x32 = x.astype(F32)
    left = jnp.where(at == 0, lead, pltpu.roll(x32, 1, 0))
    right = jnp.where(at == w - 1, tail, pltpu.roll(x32, w - 1, 0))
    return left.astype(BF16), right.astype(BF16)


def pair_of_rows(row, r, u_ref):
    def product(k, a, b, add):
        sums = [x + y if add else x - y for x, y in zip(row(r + a), row(r + b))]
        return jnp.dot(jnp.concatenate(sums, axis=1), u_ref[k], preferred_element_type=F32)

    m1 = product(1, 1, 2, True)
    m2 = product(2, 2, 1, False)
    m0 = product(0, 0, 2, False)
    m3 = product(3, 1, 3, False)
    return m0 + (m1 + m2), (m1 - m2) - m3


def finish(centre, half):
    return (centre.astype(F32) + (half + half * jnp.tanh(half))).astype(BF16)


def inner_kernel(before, here, after, u_ref, lh_ref, rh_ref, bias_ref, out_ref, sides):
    i = pl.program_id(0)
    n = here.shape[0]
    bias = bias_ref[...] * 0.5

    def centre(r):
        return before[0] if r == 0 else after[0] if r > n else here[r - 1]

    def shift(r):
        at = (i + 1) * n - 1 + r
        lead, tail = lh_ref[pl.ds(at, 1), :], rh_ref[pl.ds(at, 1), :]
        sides[r, 0], sides[r, 1] = side_columns(centre(r), lead, tail)

    def row(r):
        return sides[r, 0], centre(r), sides[r, 1]

    @pl.when(i == 0)
    def _():
        shift(0)
        shift(1)

    @pl.when(i > 0)
    def _():
        sides[0:2] = sides[n : n + 2]

    for r in range(0, n, 2):
        shift(r + 2)
        shift(r + 3)
        ya, yb = pair_of_rows(row, r, u_ref)
        out_ref[r] = finish(here[r], ya + bias)
        out_ref[r + 1] = finish(here[r + 1], yb + bias)


def edge_kernel(here, second, top, bot, u_ref, lh_ref, rh_ref, bias_ref, out_ref, ends, sides):
    i = pl.program_id(0)
    n, w, _ = here.shape
    base = i * (lh_ref.shape[0] - 16 - n)
    bias = bias_ref[...] * 0.5
    ends[0] = jnp.where(i == 0, top[0:w, :], second[0])
    ends[1] = jnp.where(i == 0, second[0], bot[0:w, :])

    def centre(r):
        return here[r - 1] if 0 < r <= n else ends[r // n]

    def shift(r):
        lead, tail = lh_ref[pl.ds(base + r, 1), :], rh_ref[pl.ds(base + r, 1), :]
        sides[r, 0], sides[r, 1] = side_columns(centre(r), lead, tail)

    def row(r):
        return sides[r, 0], centre(r), sides[r, 1]

    shift(0)
    shift(1)
    for r in range(0, n, 2):
        shift(r + 2)
        shift(r + 3)
        ya, yb = pair_of_rows(row, r, u_ref)
        out_ref[r] = finish(here[r], ya + bias)
        out_ref[r + 1] = finish(here[r + 1], yb + bias)


def ends_kernel(first, last, left, right, rows_ref, cols_ref):
    rows_ref[0] = first[0]
    rows_ref[1] = last[0]
    for r in range(left.shape[0]):
        cols_ref[0, r : r + 1, :] = left[r].astype(F32)[:1]
        cols_ref[1, r : r + 1, :] = right[r].astype(F32)[-1:]


def weights_kernel(pin_ref, tw_ref, tt_ref, po_ref, u_ref, scaled):
    pin = pin_ref[...].astype(F32)
    c = pin.shape[0]
    t0, t1, t2 = tt_ref[0:1, :], tt_ref[1:2, :], tt_ref[2:3, :]
    mid = 0.5 * (t0 + t2)
    for k, tall in enumerate((t0, mid + 0.5 * t1, mid - 0.5 * t1, t2)):
        for j in range(3):
            scaled[3 * k + j] = (pin * (tall * tw_ref[j : j + 1, :] * 0.5)).astype(BF16)
    for k in range(4):
        for j in range(3):
            u = jnp.dot(scaled[3 * k + j], po_ref[...], preferred_element_type=F32)
            u_ref[k, j * c : (j + 1) * c, :] = u.astype(BF16)


def shifted(x, axis, step):
    count = lax.axis_size(axis)
    if step > 0:
        return lax.ppermute(x, axis, [(i, i + 1) for i in range(count - 1)])
    return lax.ppermute(x, axis, [(i + 1, i) for i in range(count - 1)])


def row_halos(first, last):
    count = lax.axis_size("row")
    if count % 2:
        return shifted(last, "row", 1), shifted(first, "row", -1)
    even = lax.axis_index("row") % 2 == 0

    def swap(x, start):
        pairs = [(i, i + 1) for i in range(start, count - 1, 2)]
        return lax.ppermute(x, "row", pairs + [(b, a) for a, b in pairs])

    got = swap(jnp.where(even, last, first), 0)
    far = swap(jnp.where(even, first, last), 1)
    return jnp.where(even, far, got), jnp.where(even, got, far)


def column_halos(first, last):
    if lax.axis_size("col") == 2:
        low = lax.axis_index("col") == 0
        got = lax.ppermute(jnp.where(low, last, first), "col", [(0, 1), (1, 0)])
        zero = jnp.zeros_like(got)
        return jnp.where(low, zero, got), jnp.where(low, got, zero)
    return shifted(last, "col", 1), shifted(first, "col", -1)


def on_device(image, proj_in, taps_wide, taps_tall, proj_out, bias):
    th, w, c = image.shape
    n = ROWS

    def whole(x):
        return pl.BlockSpec(x.shape, lambda i: (0,) * len(x.shape))

    def one_row(index):
        return pl.BlockSpec((1, w, c), lambda i: (index(i), 0, 0))

    def some_columns(at):
        return pl.BlockSpec((th, 16, c), lambda i: (0, at, 0))

    params = pltpu.CompilerParams(vmem_limit_bytes=48 * MIB)
    ends = jax.ShapeDtypeStruct((2, w, c), BF16), jax.ShapeDtypeStruct((2, th, c), F32)
    rows, cols = pl.pallas_call(
        ends_kernel,
        grid=(1,),
        out_shape=ends,
        in_specs=[one_row(lambda i: 0), one_row(lambda i: th - 1),
                  some_columns(0), some_columns(w // 16 - 1)],
        out_specs=tuple(whole(x) for x in ends),
        compiler_params=params,
        name="ends",
    )(image, image, image, image)
    lh, rh = column_halos(cols[0].astype(BF16), cols[1].astype(BF16))

    def extended(k, at):
        pad = jnp.zeros((14, c), BF16)
        return jnp.concatenate([rows[k], lh[at][None], rh[at][None], pad], axis=0)

    top, bot = row_halos(extended(0, 0), extended(1, th - 1))

    args = (proj_in, taps_wide, taps_tall, proj_out)
    weights = jax.ShapeDtypeStruct((4, 3 * c, c), BF16)
    u = pl.pallas_call(
        weights_kernel,
        grid=(1,),
        out_shape=weights,
        in_specs=[whole(x) for x in args],
        out_specs=whole(weights),
        scratch_shapes=[pltpu.VMEM((12,) + proj_in.shape, BF16)],
        compiler_params=params,
        cost_estimate=pl.CostEstimate(
            flops=24 * c * c * proj_in.shape[1], bytes_accessed=3 * MIB, transcendentals=0),
        name="weights",
    )(*args)

    def column(x, at):
        pad = jnp.zeros((14, c), BF16)
        return jnp.concatenate([top[at][None], x, bot[at][None], pad], axis=0).astype(F32)

    def cost(count):
        return pl.CostEstimate(
            flops=count * 12 * w * c * c, bytes_accessed=4 * count * w * c,
            transcendentals=count * w * c)

    bias2 = bias.reshape(1, c)
    small = (u, lh.astype(F32), rh.astype(F32), bias2)
    inner = pl.pallas_call(
        inner_kernel,
        grid=(th // n - 2,),
        out_shape=jax.ShapeDtypeStruct(image.shape, BF16),
        in_specs=[
            one_row(lambda i: (i + 1) * n - 1),
            pl.BlockSpec((n, w, c), lambda i: (i + 1, 0, 0)),
            one_row(lambda i: (i + 2) * n),
            *[whole(x) for x in small],
        ],
        out_specs=pl.BlockSpec((n, w, c), lambda i: (i + 1, 0, 0)),
        scratch_shapes=[pltpu.VMEM((n + 2, 2, w, c), BF16)],
        compiler_params=params,
        cost_estimate=cost(th - 2 * n),
        name="inner",
    )(image, image, image, *small)

    small = (top, bot, u, column(lh, w), column(rh, w + 1), bias2)
    edges = pl.pallas_call(
        edge_kernel,
        grid=(2,),
        out_shape=jax.ShapeDtypeStruct((2 * n, w, c), BF16),
        in_specs=[
            pl.BlockSpec((n, w, c), lambda i: (i * (th // n - 1), 0, 0)),
            one_row(lambda i: n + i * (th - 2 * n - 1)),
            *[whole(x) for x in small],
        ],
        out_specs=pl.BlockSpec((n, w, c), lambda i: (i, 0, 0)),
        scratch_shapes=[pltpu.VMEM((2, w, c), BF16), pltpu.VMEM((n + 2, 2, w, c), BF16)],
        compiler_params=params,
        cost_estimate=cost(2 * n),
        name="edges",
    )(image, image, *small)
    out = lax.dynamic_update_slice(inner, edges[:n], (0, 0, 0))
    return lax.dynamic_update_slice(out, edges[n:], (th - n, 0, 0))


def solution(mesh):
    in_specs = (P("row", "col", None), P(), P(), P(), P(), P())
    out_specs = P("row", "col", None)
    return jax.shard_map(
        on_device, mesh=mesh, in_specs=in_specs, out_specs=out_specs, check_vma=False
    )
```

```python
import jax
import jax.numpy as jnp
from jax import lax
from jax.experimental import pallas as pl
from jax.experimental.pallas import tpu as pltpu
from jax.sharding import PartitionSpec as P

BF16 = jnp.bfloat16
F32 = jnp.float32
MIB = 1 << 20
ROWS = 8
PIECE = 128


def side_columns(x, lead, tail):
    w = x.shape[0]
    at = lax.broadcasted_iota(jnp.int32, x.shape, 0)
    x32 = x.astype(F32)
    left = jnp.where(at == 0, lead, pltpu.roll(x32, 1, 0))
    right = jnp.where(at == w - 1, tail, pltpu.roll(x32, w - 1, 0))
    return left.astype(BF16), right.astype(BF16)


def conv_kernel(before, here, after, top, bot, u_ref, lh_ref, rh_ref, bias_ref, out_ref,
                ends, sides):
    i = pl.program_id(0)
    n, w, _ = here.shape
    bias = bias_ref[...] * 0.5

    def centre(r, cols=slice(None)):
        return here[r - 1, cols] if 0 < r <= n else ends[r // n, cols]

    def shift(r):
        at = i * n + r
        lead, tail = lh_ref[pl.ds(at, 1), :], rh_ref[pl.ds(at, 1), :]
        sides[r, 0], sides[r, 1] = side_columns(centre(r), lead, tail)

    def row(r, cols):
        return sides[r, 0, cols], centre(r, cols), sides[r, 1, cols]

    def product(k, a, b, add, cols):
        sums = [x + y if add else x - y for x, y in zip(row(a, cols), row(b, cols))]
        return jnp.dot(jnp.concatenate(sums, axis=1), u_ref[k], preferred_element_type=F32)

    def finish(r, half, cols):
        x = here[r, cols].astype(F32)
        out_ref[r, cols] = (x + (half + half * jnp.tanh(half))).astype(BF16)

    ends[0] = jnp.where(i == 0, top[...], before[0])
    ends[1] = jnp.where(i == pl.num_programs(0) - 1, bot[...], after[0])
    shift(0)
    shift(1)
    for r in range(0, n, 2):
        shift(r + 2)
        shift(r + 3)
        for start in range(0, w, PIECE):
            cols = slice(start, start + PIECE)
            m1 = product(1, r + 1, r + 2, True, cols)
            m2 = product(2, r + 2, r + 1, False, cols)
            m0 = product(0, r, r + 2, False, cols)
            m3 = product(3, r + 1, r + 3, False, cols)
            finish(r, m0 + (m1 + m2) + bias, cols)
            finish(r + 1, (m1 - m2) - m3 + bias, cols)


def ends_kernel(first, last, left, right, rows_ref, cols_ref):
    rows_ref[0] = first[0]
    rows_ref[1] = last[0]
    for r in range(left.shape[0]):
        cols_ref[0, r : r + 1, :] = left[r].astype(F32)[:1]
        cols_ref[1, r : r + 1, :] = right[r].astype(F32)[-1:]


def weights_kernel(pin_ref, tw_ref, tt_ref, po_ref, u_ref, scaled):
    pin = pin_ref[...].astype(F32)
    c = pin.shape[0]
    t0, t1, t2 = tt_ref[0:1, :], tt_ref[1:2, :], tt_ref[2:3, :]
    mid = 0.5 * (t0 + t2)
    for k, tall in enumerate((t0, mid + 0.5 * t1, mid - 0.5 * t1, t2)):
        for j in range(3):
            scaled[3 * k + j] = (pin * (tall * tw_ref[j : j + 1, :] * 0.5)).astype(BF16)
    for k in range(4):
        for j in range(3):
            u = jnp.dot(scaled[3 * k + j], po_ref[...], preferred_element_type=F32)
            u_ref[k, j * c : (j + 1) * c, :] = u.astype(BF16)


def shifted(x, axis, step):
    count = lax.axis_size(axis)
    if step > 0:
        return lax.ppermute(x, axis, [(i, i + 1) for i in range(count - 1)])
    return lax.ppermute(x, axis, [(i + 1, i) for i in range(count - 1)])


def row_halos(first, last):
    count = lax.axis_size("row")
    if count % 2:
        return shifted(last, "row", 1), shifted(first, "row", -1)
    even = lax.axis_index("row") % 2 == 0

    def swap(x, start):
        pairs = [(i, i + 1) for i in range(start, count - 1, 2)]
        return lax.ppermute(x, "row", pairs + [(b, a) for a, b in pairs])

    got = swap(jnp.where(even, last, first), 0)
    far = swap(jnp.where(even, first, last), 1)
    return jnp.where(even, far, got), jnp.where(even, got, far)


def column_halos(first, last):
    if lax.axis_size("col") == 2:
        low = lax.axis_index("col") == 0
        got = lax.ppermute(jnp.where(low, last, first), "col", [(0, 1), (1, 0)])
        zero = jnp.zeros_like(got)
        return jnp.where(low, zero, got), jnp.where(low, got, zero)
    return shifted(last, "col", 1), shifted(first, "col", -1)


def on_device(image, proj_in, taps_wide, taps_tall, proj_out, bias):
    th, w, c = image.shape
    n = ROWS

    def whole(x):
        return pl.BlockSpec(x.shape, lambda i: (0,) * len(x.shape))

    def one_row(index):
        return pl.BlockSpec((1, w, c), lambda i: (index(i), 0, 0))

    def some_columns(at):
        return pl.BlockSpec((th, 16, c), lambda i: (0, at, 0))

    params = pltpu.CompilerParams(vmem_limit_bytes=48 * MIB)
    ends = jax.ShapeDtypeStruct((2, w, c), BF16), jax.ShapeDtypeStruct((2, th, c), F32)
    rows, cols = pl.pallas_call(
        ends_kernel,
        grid=(1,),
        out_shape=ends,
        in_specs=[one_row(lambda i: 0), one_row(lambda i: th - 1),
                  some_columns(0), some_columns(w // 16 - 1)],
        out_specs=tuple(whole(x) for x in ends),
        compiler_params=params,
        name="ends",
    )(image, image, image, image)
    top, bot = row_halos(rows[0], rows[1])

    args = (proj_in, taps_wide, taps_tall, proj_out)
    weights = jax.ShapeDtypeStruct((4, 3 * c, c), BF16)
    u = pl.pallas_call(
        weights_kernel,
        grid=(1,),
        out_shape=weights,
        in_specs=[whole(x) for x in args],
        out_specs=whole(weights),
        scratch_shapes=[pltpu.VMEM((12,) + proj_in.shape, BF16)],
        compiler_params=params,
        cost_estimate=pl.CostEstimate(
            flops=24 * c * c * proj_in.shape[1], bytes_accessed=3 * MIB, transcendentals=0),
        name="weights",
    )(*args)

    def column(k, at):
        pad = jnp.zeros((14, c), BF16)
        return jnp.concatenate(
            [top[at][None], cols[k].astype(BF16), bot[at][None], pad], axis=0)

    lh, rh = column_halos(column(0, 0), column(1, w - 1))
    small = (top, bot, u, lh.astype(F32), rh.astype(F32), bias.reshape(1, c))
    block = pl.BlockSpec((n, w, c), lambda i: (i, 0, 0))
    return pl.pallas_call(
        conv_kernel,
        grid=(th // n,),
        out_shape=jax.ShapeDtypeStruct(image.shape, BF16),
        in_specs=[
            one_row(lambda i: jnp.maximum(i * n - 1, 0)),
            block,
            one_row(lambda i: jnp.minimum(i * n + n, th - 1)),
            *[whole(x) for x in small],
        ],
        out_specs=block,
        scratch_shapes=[pltpu.VMEM((2, w, c), BF16), pltpu.VMEM((n + 2, 2, w, c), BF16)],
        compiler_params=params,
        name="conv",
    )(image, image, image, *small)


def solution(mesh):
    in_specs = (P("row", "col", None), P(), P(), P(), P(), P())
    out_specs = P("row", "col", None)
    return jax.shard_map(
        on_device, mesh=mesh, in_specs=in_specs, out_specs=out_specs, check_vma=False
    )
```

```python
import jax
import jax.numpy as jnp
from jax import lax
from jax.experimental import pallas as pl
from jax.experimental.pallas import tpu as pltpu
from jax.sharding import PartitionSpec as P

BF16 = jnp.bfloat16
F32 = jnp.float32
MIB = 1 << 20
ROWS = 8


def side_columns(x, lead, tail, left_ref, right_ref):
    w = x.shape[0]
    left, right = pltpu.roll(x, 1, 0), pltpu.roll(x, w - 1, 0)
    at = lax.broadcasted_iota(jnp.int32, (16, x.shape[1]), 0)
    left_ref[16:w] = left[16:]
    left_ref[0:16] = jnp.where(at == 0, lead, left[:16].astype(F32)).astype(BF16)
    right_ref[0 : w - 16] = right[: w - 16]
    right_ref[w - 16 : w] = jnp.where(at == 15, tail, right[w - 16 :].astype(F32)).astype(BF16)


def conv_kernel(before, here, after, top, bot, u_ref, lh_ref, rh_ref, bias_ref, out_ref,
                ends, sides):
    i = pl.program_id(0)
    n, w, _ = here.shape
    bias = bias_ref[...] * 0.5

    def centre(r):
        return here[r - 1] if 0 < r <= n else ends[r // n]

    def shift(r):
        at = i * n + r
        lead, tail = lh_ref[pl.ds(at, 1), :], rh_ref[pl.ds(at, 1), :]
        side_columns(centre(r), lead, tail, sides.at[r, 0], sides.at[r, 1])

    def row(r):
        return sides[r, 0], centre(r), sides[r, 1]

    def product(k, a, b, add):
        sums = [x + y if add else x - y for x, y in zip(row(a), row(b))]
        return jnp.dot(jnp.concatenate(sums, axis=1), u_ref[k], preferred_element_type=F32)

    def finish(r, half):
        x = here[r].astype(F32)
        out_ref[r] = (x + (half + half * jnp.tanh(half))).astype(BF16)

    ends[0] = jnp.where(i == 0, top[...], before[0])
    ends[1] = jnp.where(i == pl.num_programs(0) - 1, bot[...], after[0])
    shift(0)
    shift(1)
    for r in range(0, n, 2):
        shift(r + 2)
        shift(r + 3)
        m1 = product(1, r + 1, r + 2, True)
        m2 = product(2, r + 2, r + 1, False)
        m0 = product(0, r, r + 2, False)
        m3 = product(3, r + 1, r + 3, False)
        finish(r, m0 + (m1 + m2) + bias)
        finish(r + 1, (m1 - m2) - m3 + bias)


def ends_kernel(first, last, left, right, rows_ref, cols_ref):
    rows_ref[0] = first[0]
    rows_ref[1] = last[0]
    for r in range(left.shape[0]):
        cols_ref[0, r : r + 1, :] = left[r].astype(F32)[:1]
        cols_ref[1, r : r + 1, :] = right[r].astype(F32)[-1:]


def weights_kernel(pin_ref, tw_ref, tt_ref, po_ref, u_ref, scaled):
    pin = pin_ref[...].astype(F32)
    c = pin.shape[0]
    t0, t1, t2 = tt_ref[0:1, :], tt_ref[1:2, :], tt_ref[2:3, :]
    mid = 0.5 * (t0 + t2)
    for k, tall in enumerate((t0, mid + 0.5 * t1, mid - 0.5 * t1, t2)):
        for j in range(3):
            scaled[3 * k + j] = (pin * (tall * tw_ref[j : j + 1, :] * 0.5)).astype(BF16)
    for k in range(4):
        for j in range(3):
            u = jnp.dot(scaled[3 * k + j], po_ref[...], preferred_element_type=F32)
            u_ref[k, j * c : (j + 1) * c, :] = u.astype(BF16)


def shifted(x, axis, step):
    count = lax.axis_size(axis)
    if step > 0:
        return lax.ppermute(x, axis, [(i, i + 1) for i in range(count - 1)])
    return lax.ppermute(x, axis, [(i + 1, i) for i in range(count - 1)])


def row_halos(first, last):
    count = lax.axis_size("row")
    if count % 2:
        return shifted(last, "row", 1), shifted(first, "row", -1)
    even = lax.axis_index("row") % 2 == 0

    def swap(x, start):
        pairs = [(i, i + 1) for i in range(start, count - 1, 2)]
        return lax.ppermute(x, "row", pairs + [(b, a) for a, b in pairs])

    got = swap(jnp.where(even, last, first), 0)
    far = swap(jnp.where(even, first, last), 1)
    return jnp.where(even, far, got), jnp.where(even, got, far)


def column_halos(first, last):
    if lax.axis_size("col") == 2:
        low = lax.axis_index("col") == 0
        got = lax.ppermute(jnp.where(low, last, first), "col", [(0, 1), (1, 0)])
        zero = jnp.zeros_like(got)
        return jnp.where(low, zero, got), jnp.where(low, got, zero)
    return shifted(last, "col", 1), shifted(first, "col", -1)


def on_device(image, proj_in, taps_wide, taps_tall, proj_out, bias):
    th, w, c = image.shape
    n = ROWS

    def whole(x):
        return pl.BlockSpec(x.shape, lambda i: (0,) * len(x.shape))

    def one_row(index):
        return pl.BlockSpec((1, w, c), lambda i: (index(i), 0, 0))

    def some_columns(at):
        return pl.BlockSpec((th, 16, c), lambda i: (0, at, 0))

    params = pltpu.CompilerParams(vmem_limit_bytes=48 * MIB)
    ends = jax.ShapeDtypeStruct((2, w, c), BF16), jax.ShapeDtypeStruct((2, th, c), F32)
    rows, cols = pl.pallas_call(
        ends_kernel,
        grid=(1,),
        out_shape=ends,
        in_specs=[one_row(lambda i: 0), one_row(lambda i: th - 1),
                  some_columns(0), some_columns(w // 16 - 1)],
        out_specs=tuple(whole(x) for x in ends),
        compiler_params=params,
        name="ends",
    )(image, image, image, image)
    top, bot = row_halos(rows[0], rows[1])

    args = (proj_in, taps_wide, taps_tall, proj_out)
    weights = jax.ShapeDtypeStruct((4, 3 * c, c), BF16)
    u = pl.pallas_call(
        weights_kernel,
        grid=(1,),
        out_shape=weights,
        in_specs=[whole(x) for x in args],
        out_specs=whole(weights),
        scratch_shapes=[pltpu.VMEM((12,) + proj_in.shape, BF16)],
        compiler_params=params,
        cost_estimate=pl.CostEstimate(
            flops=24 * c * c * proj_in.shape[1], bytes_accessed=3 * MIB, transcendentals=0),
        name="weights",
    )(*args)

    def column(k, at):
        pad = jnp.zeros((14, c), BF16)
        return jnp.concatenate(
            [top[at][None], cols[k].astype(BF16), bot[at][None], pad], axis=0)

    lh, rh = column_halos(column(0, 0), column(1, w - 1))
    small = (top, bot, u, lh.astype(F32), rh.astype(F32), bias.reshape(1, c))
    block = pl.BlockSpec((n, w, c), lambda i: (i, 0, 0))
    return pl.pallas_call(
        conv_kernel,
        grid=(th // n,),
        out_shape=jax.ShapeDtypeStruct(image.shape, BF16),
        in_specs=[
            one_row(lambda i: jnp.maximum(i * n - 1, 0)),
            block,
            one_row(lambda i: jnp.minimum(i * n + n, th - 1)),
            *[whole(x) for x in small],
        ],
        out_specs=block,
        scratch_shapes=[pltpu.VMEM((2, w, c), BF16), pltpu.VMEM((n + 2, 2, w, c), BF16)],
        compiler_params=params,
        name="conv",
    )(image, image, image, *small)


def solution(mesh):
    in_specs = (P("row", "col", None), P(), P(), P(), P(), P())
    out_specs = P("row", "col", None)
    return jax.shard_map(
        on_device, mesh=mesh, in_specs=in_specs, out_specs=out_specs, check_vma=False
    )
```

```python
import jax
import jax.numpy as jnp
from jax import lax
from jax.experimental import pallas as pl
from jax.experimental.pallas import tpu as pltpu
from jax.sharding import PartitionSpec as P

BF16 = jnp.bfloat16
F32 = jnp.float32
MIB = 1 << 20
ROWS = 8


def with_sides(x, lead, tail):
    w = x.shape[0]
    left, right = pltpu.roll(x, 1, 0), pltpu.roll(x, w - 1, 0)
    at = lax.broadcasted_iota(jnp.int32, (16, x.shape[1]), 0)
    head = jnp.where(at == 0, lead, left[:16].astype(F32)).astype(BF16)
    foot = jnp.where(at == 15, tail, right[w - 16 :].astype(F32)).astype(BF16)
    left = jnp.concatenate([head, left[16:]], axis=0)
    right = jnp.concatenate([right[: w - 16], foot], axis=0)
    return jnp.concatenate([left, x, right], axis=1)


def conv_kernel(before, here, after, top, bot, u_ref, lh_ref, rh_ref, bias_ref, out_ref,
                ends):
    i = pl.program_id(0)
    n, w, _ = here.shape
    bias = bias_ref[...] * 0.5

    def centre(r):
        return here[r - 1] if 0 < r <= n else ends[r // n]

    def product(k, a, b, add):
        def both(x, y):
            return x + y if add else x - y

        lead, tail = [
            both(ref[pl.ds(i * n + a, 1), :], ref[pl.ds(i * n + b, 1), :]) for ref in (lh_ref, rh_ref)
        ]
        lhs = with_sides(both(centre(a), centre(b)), lead, tail)
        return jnp.dot(lhs, u_ref[k], preferred_element_type=F32)

    def finish(r, half):
        x = here[r].astype(F32)
        out_ref[r] = (x + (half + half * jnp.tanh(half))).astype(BF16)

    ends[0] = jnp.where(i == 0, top[...], before[0])
    ends[1] = jnp.where(i == pl.num_programs(0) - 1, bot[...], after[0])
    for r in range(0, n, 2):
        m1 = product(1, r + 1, r + 2, True)
        m2 = product(2, r + 2, r + 1, False)
        m0 = product(0, r, r + 2, False)
        m3 = product(3, r + 1, r + 3, False)
        finish(r, m0 + (m1 + m2) + bias)
        finish(r + 1, (m1 - m2) - m3 + bias)


def ends_kernel(first, last, left, right, rows_ref, cols_ref):
    rows_ref[0] = first[0]
    rows_ref[1] = last[0]
    for r in range(left.shape[0]):
        cols_ref[0, r : r + 1, :] = left[r].astype(F32)[:1]
        cols_ref[1, r : r + 1, :] = right[r].astype(F32)[-1:]


def weights_kernel(pin_ref, tw_ref, tt_ref, po_ref, u_ref, scaled):
    pin = pin_ref[...].astype(F32)
    c = pin.shape[0]
    t0, t1, t2 = tt_ref[0:1, :], tt_ref[1:2, :], tt_ref[2:3, :]
    mid = 0.5 * (t0 + t2)
    for k, tall in enumerate((t0, mid + 0.5 * t1, mid - 0.5 * t1, t2)):
        for j in range(3):
            scaled[3 * k + j] = (pin * (tall * tw_ref[j : j + 1, :] * 0.5)).astype(BF16)
    for k in range(4):
        for j in range(3):
            u = jnp.dot(scaled[3 * k + j], po_ref[...], preferred_element_type=F32)
            u_ref[k, j * c : (j + 1) * c, :] = u.astype(BF16)


def shifted(x, axis, step):
    count = lax.axis_size(axis)
    if step > 0:
        return lax.ppermute(x, axis, [(i, i + 1) for i in range(count - 1)])
    return lax.ppermute(x, axis, [(i + 1, i) for i in range(count - 1)])


def row_halos(first, last):
    count = lax.axis_size("row")
    if count % 2:
        return shifted(last, "row", 1), shifted(first, "row", -1)
    even = lax.axis_index("row") % 2 == 0

    def swap(x, start):
        pairs = [(i, i + 1) for i in range(start, count - 1, 2)]
        return lax.ppermute(x, "row", pairs + [(b, a) for a, b in pairs])

    got = swap(jnp.where(even, last, first), 0)
    far = swap(jnp.where(even, first, last), 1)
    return jnp.where(even, far, got), jnp.where(even, got, far)


def column_halos(first, last):
    if lax.axis_size("col") == 2:
        low = lax.axis_index("col") == 0
        got = lax.ppermute(jnp.where(low, last, first), "col", [(0, 1), (1, 0)])
        zero = jnp.zeros_like(got)
        return jnp.where(low, zero, got), jnp.where(low, got, zero)
    return shifted(last, "col", 1), shifted(first, "col", -1)


def on_device(image, proj_in, taps_wide, taps_tall, proj_out, bias):
    th, w, c = image.shape
    n = ROWS

    def whole(x):
        return pl.BlockSpec(x.shape, lambda i: (0,) * len(x.shape))

    def one_row(index):
        return pl.BlockSpec((1, w, c), lambda i: (index(i), 0, 0))

    def some_columns(at):
        return pl.BlockSpec((th, 16, c), lambda i: (0, at, 0))

    params = pltpu.CompilerParams(vmem_limit_bytes=48 * MIB)
    ends = jax.ShapeDtypeStruct((2, w, c), BF16), jax.ShapeDtypeStruct((2, th, c), F32)
    rows, cols = pl.pallas_call(
        ends_kernel,
        grid=(1,),
        out_shape=ends,
        in_specs=[one_row(lambda i: 0), one_row(lambda i: th - 1),
                  some_columns(0), some_columns(w // 16 - 1)],
        out_specs=tuple(whole(x) for x in ends),
        compiler_params=params,
        name="ends",
    )(image, image, image, image)
    top, bot = row_halos(rows[0], rows[1])

    args = (proj_in, taps_wide, taps_tall, proj_out)
    weights = jax.ShapeDtypeStruct((4, 3 * c, c), BF16)
    u = pl.pallas_call(
        weights_kernel,
        grid=(1,),
        out_shape=weights,
        in_specs=[whole(x) for x in args],
        out_specs=whole(weights),
        scratch_shapes=[pltpu.VMEM((12,) + proj_in.shape, BF16)],
        compiler_params=params,
        cost_estimate=pl.CostEstimate(
            flops=24 * c * c * proj_in.shape[1], bytes_accessed=3 * MIB, transcendentals=0),
        name="weights",
    )(*args)

    def column(k, at):
        pad = jnp.zeros((14, c), BF16)
        return jnp.concatenate(
            [top[at][None], cols[k].astype(BF16), bot[at][None], pad], axis=0)

    lh, rh = column_halos(column(0, 0), column(1, w - 1))
    small = (top, bot, u, lh.astype(F32), rh.astype(F32), bias.reshape(1, c))
    block = pl.BlockSpec((n, w, c), lambda i: (i, 0, 0))
    return pl.pallas_call(
        conv_kernel,
        grid=(th // n,),
        out_shape=jax.ShapeDtypeStruct(image.shape, BF16),
        in_specs=[
            one_row(lambda i: jnp.maximum(i * n - 1, 0)),
            block,
            one_row(lambda i: jnp.minimum(i * n + n, th - 1)),
            *[whole(x) for x in small],
        ],
        out_specs=block,
        scratch_shapes=[pltpu.VMEM((2, w, c), BF16)],
        compiler_params=params,
        name="conv",
    )(image, image, image, *small)


def solution(mesh):
    in_specs = (P("row", "col", None), P(), P(), P(), P(), P())
    out_specs = P("row", "col", None)
    return jax.shard_map(
        on_device, mesh=mesh, in_specs=in_specs, out_specs=out_specs, check_vma=False
    )
```

```python
import jax
import jax.numpy as jnp
from jax import lax
from jax.experimental import pallas as pl
from jax.experimental.pallas import tpu as pltpu
from jax.sharding import PartitionSpec as P

BF16 = jnp.bfloat16
F32 = jnp.float32
MIB = 1 << 20
ROWS = 8


def with_sides(x, lead, tail):
    w = x.shape[0]
    left, right = pltpu.roll(x, 1, 0), pltpu.roll(x, w - 1, 0)
    at = lax.broadcasted_iota(jnp.int32, (16, x.shape[1]), 0)
    head = jnp.where(at == 0, lead, left[:16].astype(F32)).astype(BF16)
    foot = jnp.where(at == 15, tail, right[w - 16 :].astype(F32)).astype(BF16)
    left = jnp.concatenate([head, left[16:]], axis=0)
    right = jnp.concatenate([right[: w - 16], foot], axis=0)
    return jnp.concatenate([left, x, right], axis=1)


def conv_kernel(before, here, after, top, bot, u_ref, lh_ref, rh_ref, bias_ref, out_ref,
                ends):
    i = pl.program_id(0)
    n, w, _ = here.shape
    bias = bias_ref[...] * 0.5

    def centre(r):
        return here[r - 1] if 0 < r <= n else ends[r // n]

    def product(k, a, b, add):
        def both(x, y):
            return x + y if add else x - y

        lead, tail = [
            both(ref[pl.ds(i * n + a, 1), :], ref[pl.ds(i * n + b, 1), :]) for ref in (lh_ref, rh_ref)
        ]
        lhs = with_sides(both(centre(a), centre(b)), lead, tail)
        return jnp.dot(lhs, u_ref[k], preferred_element_type=F32)

    def finish(r, half):
        x = here[r].astype(F32)
        out_ref[r] = (x + (half + half * jnp.tanh(half))).astype(BF16)

    ends[0] = jnp.where(i == 0, top[...], before[0])
    ends[1] = jnp.where(i == pl.num_programs(0) - 1, bot[...], after[0])
    for r in range(0, n, 2):
        m1 = product(1, r + 1, r + 2, True)
        m2 = product(2, r + 2, r + 1, False)
        m0 = product(0, r, r + 2, False)
        m3 = product(3, r + 1, r + 3, False)
        finish(r, m0 + (m1 + m2) + bias)
        finish(r + 1, (m1 - m2) - m3 + bias)


def ends_kernel(first, last, left, right, rows_ref, cols_ref):
    rows_ref[0] = first[0]
    rows_ref[1] = last[0]
    for r in range(left.shape[0]):
        cols_ref[0, r : r + 1, :] = left[r].astype(F32)[:1]
        cols_ref[1, r : r + 1, :] = right[r].astype(F32)[-1:]


def weights_kernel(pin_ref, tw_ref, tt_ref, po_ref, u_ref, scaled):
    pin = pin_ref[...].astype(F32)
    c = pin.shape[0]
    t0, t1, t2 = tt_ref[0:1, :], tt_ref[1:2, :], tt_ref[2:3, :]
    mid = 0.5 * (t0 + t2)
    for k, tall in enumerate((t0, mid + 0.5 * t1, mid - 0.5 * t1, t2)):
        for j in range(3):
            scaled[3 * k + j] = (pin * (tall * tw_ref[j : j + 1, :] * 0.5)).astype(BF16)
    for k in range(4):
        for j in range(3):
            u = jnp.dot(scaled[3 * k + j], po_ref[...], preferred_element_type=F32)
            u_ref[k, j * c : (j + 1) * c, :] = u.astype(BF16)


def shifted(x, axis, step):
    count = lax.axis_size(axis)
    if step > 0:
        return lax.ppermute(x, axis, [(i, i + 1) for i in range(count - 1)])
    return lax.ppermute(x, axis, [(i + 1, i) for i in range(count - 1)])


def row_swap(x, start, cross=False):
    ends = range(start, lax.axis_size("row") - 1, 2)
    pairs = [(i, i + 1) for i in ends]
    axis = "row"
    if cross:
        pairs = [(2 * i + k, 2 * (i + 1) + 1 - k) for i in ends for k in range(2)]
        axis = ("row", "col")
    return lax.ppermute(x, axis, pairs + [(b, a) for a, b in pairs])


def row_halos(first, last):
    if lax.axis_size("row") % 2:
        return shifted(last, "row", 1), shifted(first, "row", -1)
    even = lax.axis_index("row") % 2 == 0
    got = row_swap(jnp.where(even, last, first), 0)
    far = row_swap(jnp.where(even, first, last), 1)
    return jnp.where(even, far, got), jnp.where(even, got, far)


def columns_of_two(first, last):
    even, low = lax.axis_index("row") % 2 == 0, lax.axis_index("col") == 0
    side = jnp.where(low, last, first)
    head, foot = side[:16], side[-16:]
    mid = lax.ppermute(side, "col", [(0, 1), (1, 0)])
    got = row_swap(jnp.where(even, foot, head), 0, True)
    far = row_swap(jnp.where(even, head, foot), 1, True)
    up = jnp.where(even, far[15:], got[15:])
    down = jnp.where(even, got[:1], far[:1])
    pad = jnp.zeros((14, side.shape[1]), BF16)
    column = jnp.concatenate([up, mid, down, pad], axis=0).astype(F32)
    zero = jnp.zeros_like(column)
    return jnp.where(low, zero, column), jnp.where(low, column, zero)


def column_halos(first, last):
    return shifted(last, "col", 1), shifted(first, "col", -1)


def on_device(image, proj_in, taps_wide, taps_tall, proj_out, bias):
    th, w, c = image.shape
    n = ROWS

    def whole(x):
        return pl.BlockSpec(x.shape, lambda i: (0,) * len(x.shape))

    def one_row(index):
        return pl.BlockSpec((1, w, c), lambda i: (index(i), 0, 0))

    def some_columns(at):
        return pl.BlockSpec((th, 16, c), lambda i: (0, at, 0))

    params = pltpu.CompilerParams(vmem_limit_bytes=48 * MIB)
    ends = jax.ShapeDtypeStruct((2, w, c), BF16), jax.ShapeDtypeStruct((2, th, c), F32)
    rows, cols = pl.pallas_call(
        ends_kernel,
        grid=(1,),
        out_shape=ends,
        in_specs=[one_row(lambda i: 0), one_row(lambda i: th - 1),
                  some_columns(0), some_columns(w // 16 - 1)],
        out_specs=tuple(whole(x) for x in ends),
        compiler_params=params,
        name="ends",
    )(image, image, image, image)
    top, bot = row_halos(rows[0], rows[1])

    args = (proj_in, taps_wide, taps_tall, proj_out)
    weights = jax.ShapeDtypeStruct((4, 3 * c, c), BF16)
    u = pl.pallas_call(
        weights_kernel,
        grid=(1,),
        out_shape=weights,
        in_specs=[whole(x) for x in args],
        out_specs=whole(weights),
        scratch_shapes=[pltpu.VMEM((12,) + proj_in.shape, BF16)],
        compiler_params=params,
        cost_estimate=pl.CostEstimate(
            flops=24 * c * c * proj_in.shape[1], bytes_accessed=3 * MIB, transcendentals=0),
        name="weights",
    )(*args)

    def column(k, at):
        pad = jnp.zeros((14, c), BF16)
        return jnp.concatenate(
            [top[at][None], cols[k].astype(BF16), bot[at][None], pad], axis=0)

    if lax.axis_size("col") == 2 and lax.axis_size("row") % 2 == 0:
        lh, rh = columns_of_two(cols[0].astype(BF16), cols[1].astype(BF16))
    else:
        lh, rh = column_halos(column(0, 0), column(1, w - 1))
    small = (top, bot, u, lh.astype(F32), rh.astype(F32), bias.reshape(1, c))
    block = pl.BlockSpec((n, w, c), lambda i: (i, 0, 0))
    return pl.pallas_call(
        conv_kernel,
        grid=(th // n,),
        out_shape=jax.ShapeDtypeStruct(image.shape, BF16),
        in_specs=[
            one_row(lambda i: jnp.maximum(i * n - 1, 0)),
            block,
            one_row(lambda i: jnp.minimum(i * n + n, th - 1)),
            *[whole(x) for x in small],
        ],
        out_specs=block,
        scratch_shapes=[pltpu.VMEM((2, w, c), BF16)],
        compiler_params=params,
        name="conv",
    )(image, image, image, *small)


def solution(mesh):
    in_specs = (P("row", "col", None), P(), P(), P(), P(), P())
    out_specs = P("row", "col", None)
    return jax.shard_map(
        on_device, mesh=mesh, in_specs=in_specs, out_specs=out_specs, check_vma=False
    )
```

```python
import jax
import jax.numpy as jnp
from jax import lax
from jax.experimental import pallas as pl
from jax.experimental.pallas import tpu as pltpu
from jax.sharding import PartitionSpec as P

BF16 = jnp.bfloat16
F32 = jnp.float32
MIB = 1 << 20
ROWS = 8


def with_sides(x, lead, tail):
    w = x.shape[0]
    left, right = pltpu.roll(x, 1, 0), pltpu.roll(x, w - 1, 0)
    at = lax.broadcasted_iota(jnp.int32, (16, x.shape[1]), 0)
    head = jnp.where(at == 0, lead, left[:16].astype(F32)).astype(BF16)
    foot = jnp.where(at == 15, tail, right[w - 16 :].astype(F32)).astype(BF16)
    left = jnp.concatenate([head, left[16:]], axis=0)
    right = jnp.concatenate([right[: w - 16], foot], axis=0)
    return left, x, right


def conv_kernel(before, here, after, top, bot, u_ref, lh_ref, rh_ref, bias_ref, out_ref,
                ends):
    i = pl.program_id(0)
    n, w, _ = here.shape
    bias = bias_ref[...] * 0.5

    def centre(r):
        return here[r - 1] if 0 < r <= n else ends[r // n]

    def product(k, a, b, add):
        def both(x, y):
            return x + y if add else x - y

        lead, tail = [
            both(ref[pl.ds(i * n + a, 1), :], ref[pl.ds(i * n + b, 1), :]) for ref in (lh_ref, rh_ref)
        ]
        lhs = with_sides(both(centre(a), centre(b)), lead, tail)
        c = u_ref.shape[2]
        parts = [
            jnp.dot(x, u_ref[k, j * c : (j + 1) * c, :], preferred_element_type=F32)
            for j, x in enumerate(lhs)
        ]
        return parts[0] + parts[1] + parts[2]

    def finish(r, half):
        x = here[r].astype(F32)
        out_ref[r] = (x + (half + half * jnp.tanh(half))).astype(BF16)

    ends[0] = jnp.where(i == 0, top[...], before[0])
    ends[1] = jnp.where(i == pl.num_programs(0) - 1, bot[...], after[0])
    for r in range(0, n, 2):
        m1 = product(1, r + 1, r + 2, True)
        m2 = product(2, r + 2, r + 1, False)
        m0 = product(0, r, r + 2, False)
        m3 = product(3, r + 1, r + 3, False)
        finish(r, m0 + (m1 + m2) + bias)
        finish(r + 1, (m1 - m2) - m3 + bias)


def rows_kernel(first, last, rows_ref):
    rows_ref[0] = first[0]
    rows_ref[1] = last[0]


def columns_kernel(left, right, cols_ref):
    for r in range(left.shape[0]):
        cols_ref[0, r : r + 1, :] = left[r].astype(F32)[:1]
        cols_ref[1, r : r + 1, :] = right[r].astype(F32)[-1:]


def weights_kernel(pin_ref, tw_ref, tt_ref, po_ref, u_ref, scaled):
    pin = pin_ref[...].astype(F32)
    c = pin.shape[0]
    t0, t1, t2 = tt_ref[0:1, :], tt_ref[1:2, :], tt_ref[2:3, :]
    mid = 0.5 * (t0 + t2)
    for k, tall in enumerate((t0, mid + 0.5 * t1, mid - 0.5 * t1, t2)):
        for j in range(3):
            scaled[3 * k + j] = (pin * (tall * tw_ref[j : j + 1, :] * 0.5)).astype(BF16)
    for k in range(4):
        for j in range(3):
            u = jnp.dot(scaled[3 * k + j], po_ref[...], preferred_element_type=F32)
            u_ref[k, j * c : (j + 1) * c, :] = u.astype(BF16)


def shifted(x, axis, step):
    count = lax.axis_size(axis)
    if step > 0:
        return lax.ppermute(x, axis, [(i, i + 1) for i in range(count - 1)])
    return lax.ppermute(x, axis, [(i + 1, i) for i in range(count - 1)])


def row_halos(first, last):
    count = lax.axis_size("row")
    if count % 2:
        return shifted(last, "row", 1), shifted(first, "row", -1)
    even = lax.axis_index("row") % 2 == 0

    def swap(x, start):
        pairs = [(i, i + 1) for i in range(start, count - 1, 2)]
        return lax.ppermute(x, "row", pairs + [(b, a) for a, b in pairs])

    got = swap(jnp.where(even, last, first), 0)
    far = swap(jnp.where(even, first, last), 1)
    return jnp.where(even, far, got), jnp.where(even, got, far)


def column_halos(first, last):
    if lax.axis_size("col") == 2:
        low = lax.axis_index("col") == 0
        got = lax.ppermute(jnp.where(low, last, first), "col", [(0, 1), (1, 0)])
        zero = jnp.zeros_like(got)
        return jnp.where(low, zero, got), jnp.where(low, got, zero)
    return shifted(last, "col", 1), shifted(first, "col", -1)


def on_device(image, proj_in, taps_wide, taps_tall, proj_out, bias):
    th, w, c = image.shape
    n = ROWS

    def whole(x):
        return pl.BlockSpec(x.shape, lambda i: (0,) * len(x.shape))

    def one_row(index):
        return pl.BlockSpec((1, w, c), lambda i: (index(i), 0, 0))

    def some_columns(at):
        return pl.BlockSpec((th, 16, c), lambda i: (0, at, 0))

    params = pltpu.CompilerParams(vmem_limit_bytes=48 * MIB)
    rows = jax.ShapeDtypeStruct((2, w, c), BF16)
    rows = pl.pallas_call(
        rows_kernel,
        grid=(1,),
        out_shape=rows,
        in_specs=[one_row(lambda i: 0), one_row(lambda i: th - 1)],
        out_specs=whole(rows),
        compiler_params=params,
        name="rows",
    )(image, image)
    top, bot = row_halos(rows[0], rows[1])

    cols = jax.ShapeDtypeStruct((2, th, c), F32)
    cols = pl.pallas_call(
        columns_kernel,
        grid=(1,),
        out_shape=cols,
        in_specs=[some_columns(0), some_columns(w // 16 - 1)],
        out_specs=whole(cols),
        compiler_params=params,
        cost_estimate=pl.CostEstimate(flops=0, bytes_accessed=3 * MIB, transcendentals=0),
        name="columns",
    )(image, image)

    args = (proj_in, taps_wide, taps_tall, proj_out)
    weights = jax.ShapeDtypeStruct((4, 3 * c, c), BF16)
    u = pl.pallas_call(
        weights_kernel,
        grid=(1,),
        out_shape=weights,
        in_specs=[whole(x) for x in args],
        out_specs=whole(weights),
        scratch_shapes=[pltpu.VMEM((12,) + proj_in.shape, BF16)],
        compiler_params=params,
        cost_estimate=pl.CostEstimate(
            flops=24 * c * c * proj_in.shape[1], bytes_accessed=3 * MIB, transcendentals=0),
        name="weights",
    )(*args)

    def column(k, at):
        pad = jnp.zeros((14, c), BF16)
        return jnp.concatenate(
            [top[at][None], cols[k].astype(BF16), bot[at][None], pad], axis=0)

    lh, rh = column_halos(column(0, 0), column(1, w - 1))
    small = (top, bot, u, lh.astype(F32), rh.astype(F32), bias.reshape(1, c))
    block = pl.BlockSpec((n, w, c), lambda i: (i, 0, 0))
    return pl.pallas_call(
        conv_kernel,
        grid=(th // n,),
        out_shape=jax.ShapeDtypeStruct(image.shape, BF16),
        in_specs=[
            one_row(lambda i: jnp.maximum(i * n - 1, 0)),
            block,
            one_row(lambda i: jnp.minimum(i * n + n, th - 1)),
            *[whole(x) for x in small],
        ],
        out_specs=block,
        scratch_shapes=[pltpu.VMEM((2, w, c), BF16)],
        compiler_params=params,
        name="conv",
    )(image, image, image, *small)


def solution(mesh):
    in_specs = (P("row", "col", None), P(), P(), P(), P(), P())
    out_specs = P("row", "col", None)
    return jax.shard_map(
        on_device, mesh=mesh, in_specs=in_specs, out_specs=out_specs, check_vma=False
    )
```

```python
import jax
import jax.numpy as jnp
from jax import lax
from jax.experimental import pallas as pl
from jax.experimental.pallas import tpu as pltpu
from jax.sharding import PartitionSpec as P

BF16 = jnp.bfloat16
F32 = jnp.float32
MIB = 1 << 20
ROWS = 4


def with_sides(x, lead, tail):
    w = x.shape[0]
    left, right = pltpu.roll(x, 1, 0), pltpu.roll(x, w - 1, 0)
    at = lax.broadcasted_iota(jnp.int32, (16, x.shape[1]), 0)
    head = jnp.where(at == 0, lead, left[:16].astype(F32)).astype(BF16)
    foot = jnp.where(at == 15, tail, right[w - 16 :].astype(F32)).astype(BF16)
    left = jnp.concatenate([head, left[16:]], axis=0)
    right = jnp.concatenate([right[: w - 16], foot], axis=0)
    return jnp.concatenate([left, x, right], axis=1)


def write_block(here, centre, base, u_ref, lh_ref, rh_ref, bias_ref, out_ref):
    bias = bias_ref[...] * 0.5

    def product(k, a, b, add):
        def both(x, y):
            return x + y if add else x - y

        lead, tail = [
            both(ref[pl.ds(base + a, 1), :], ref[pl.ds(base + b, 1), :]) for ref in (lh_ref, rh_ref)
        ]
        lhs = with_sides(both(centre(a), centre(b)), lead, tail)
        return jnp.dot(lhs, u_ref[k], preferred_element_type=F32)

    def finish(r, half):
        x = here[r].astype(F32)
        out_ref[r] = (x + (half + half * jnp.tanh(half))).astype(BF16)

    for r in range(0, here.shape[0], 2):
        m1 = product(1, r + 1, r + 2, True)
        m2 = product(2, r + 2, r + 1, False)
        m0 = product(0, r, r + 2, False)
        m3 = product(3, r + 1, r + 3, False)
        finish(r, m0 + (m1 + m2) + bias)
        finish(r + 1, (m1 - m2) - m3 + bias)


def inner_kernel(before, here, after, u_ref, lh_ref, rh_ref, bias_ref, out_ref):
    n = here.shape[0]

    def centre(r):
        return before[0] if r == 0 else after[0] if r > n else here[r - 1]

    base = (pl.program_id(0) + 1) * n - 1
    write_block(here, centre, base, u_ref, lh_ref, rh_ref, bias_ref, out_ref)


def edge_kernel(here, second, top, bot, u_ref, lh_ref, rh_ref, bias_ref, out_ref, ends):
    i = pl.program_id(0)
    n, w, _ = here.shape
    ends[0] = jnp.where(i == 0, top[0:w, :], second[0])
    ends[1] = jnp.where(i == 0, second[0], bot[0:w, :])

    def centre(r):
        return here[r - 1] if 0 < r <= n else ends[r // n]

    base = i * (lh_ref.shape[0] - 16 - n)
    write_block(here, centre, base, u_ref, lh_ref, rh_ref, bias_ref, out_ref)


def rows_kernel(first, last, rows_ref):
    rows_ref[0] = first[0]
    rows_ref[1] = last[0]


def columns_kernel(left, right, cols_ref):
    for r in range(left.shape[0]):
        cols_ref[0, r : r + 1, :] = left[r].astype(F32)[:1]
        cols_ref[1, r : r + 1, :] = right[r].astype(F32)[-1:]


def weights_kernel(pin_ref, tw_ref, tt_ref, po_ref, u_ref, scaled):
    pin = pin_ref[...].astype(F32)
    c = pin.shape[0]
    t0, t1, t2 = tt_ref[0:1, :], tt_ref[1:2, :], tt_ref[2:3, :]
    mid = 0.5 * (t0 + t2)
    for k, tall in enumerate((t0, mid + 0.5 * t1, mid - 0.5 * t1, t2)):
        for j in range(3):
            scaled[3 * k + j] = (pin * (tall * tw_ref[j : j + 1, :] * 0.5)).astype(BF16)
    for k in range(4):
        for j in range(3):
            u = jnp.dot(scaled[3 * k + j], po_ref[...], preferred_element_type=F32)
            u_ref[k, j * c : (j + 1) * c, :] = u.astype(BF16)


def shifted(x, axis, step):
    count = lax.axis_size(axis)
    if step > 0:
        return lax.ppermute(x, axis, [(i, i + 1) for i in range(count - 1)])
    return lax.ppermute(x, axis, [(i + 1, i) for i in range(count - 1)])


def row_halos(first, last):
    count = lax.axis_size("row")
    if count % 2:
        return shifted(last, "row", 1), shifted(first, "row", -1)
    even = lax.axis_index("row") % 2 == 0

    def swap(x, start):
        pairs = [(i, i + 1) for i in range(start, count - 1, 2)]
        return lax.ppermute(x, "row", pairs + [(b, a) for a, b in pairs])

    got = swap(jnp.where(even, last, first), 0)
    far = swap(jnp.where(even, first, last), 1)
    return jnp.where(even, far, got), jnp.where(even, got, far)


def column_halos(first, last):
    if lax.axis_size("col") == 2:
        low = lax.axis_index("col") == 0
        got = lax.ppermute(jnp.where(low, last, first), "col", [(0, 1), (1, 0)])
        zero = jnp.zeros_like(got)
        return jnp.where(low, zero, got), jnp.where(low, got, zero)
    return shifted(last, "col", 1), shifted(first, "col", -1)


def on_device(image, proj_in, taps_wide, taps_tall, proj_out, bias):
    th, w, c = image.shape
    n = ROWS

    def whole(x):
        return pl.BlockSpec(x.shape, lambda i: (0,) * len(x.shape))

    def one_row(index):
        return pl.BlockSpec((1, w, c), lambda i: (index(i), 0, 0))

    def some_columns(at):
        return pl.BlockSpec((th, 16, c), lambda i: (0, at, 0))

    params = pltpu.CompilerParams(vmem_limit_bytes=48 * MIB)
    cols = jax.ShapeDtypeStruct((2, th, c), F32)
    cols = pl.pallas_call(
        columns_kernel,
        grid=(1,),
        out_shape=cols,
        in_specs=[some_columns(0), some_columns(w // 16 - 1)],
        out_specs=whole(cols),
        compiler_params=params,
        cost_estimate=pl.CostEstimate(flops=0, bytes_accessed=3 * MIB, transcendentals=0),
        name="columns",
    )(image, image)

    rows = jax.ShapeDtypeStruct((2, w, c), BF16)
    rows = pl.pallas_call(
        rows_kernel,
        grid=(1,),
        out_shape=rows,
        in_specs=[one_row(lambda i: 0), one_row(lambda i: th - 1)],
        out_specs=whole(rows),
        compiler_params=params,
        cost_estimate=pl.CostEstimate(flops=0, bytes_accessed=3 * MIB, transcendentals=0),
        name="rows",
    )(image, image)
    lh, rh = column_halos(cols[0].astype(BF16), cols[1].astype(BF16))

    def extended(k, at):
        pad = jnp.zeros((14, c), BF16)
        return jnp.concatenate([rows[k], lh[at][None], rh[at][None], pad], axis=0)

    top, bot = row_halos(extended(0, 0), extended(1, th - 1))

    args = (proj_in, taps_wide, taps_tall, proj_out)
    weights = jax.ShapeDtypeStruct((4, 3 * c, c), BF16)
    u = pl.pallas_call(
        weights_kernel,
        grid=(1,),
        out_shape=weights,
        in_specs=[whole(x) for x in args],
        out_specs=whole(weights),
        scratch_shapes=[pltpu.VMEM((12,) + proj_in.shape, BF16)],
        compiler_params=params,
        cost_estimate=pl.CostEstimate(
            flops=24 * c * c * proj_in.shape[1], bytes_accessed=3 * MIB, transcendentals=0),
        name="weights",
    )(*args)

    def column(x, at):
        pad = jnp.zeros((14, c), BF16)
        return jnp.concatenate([top[at][None], x, bot[at][None], pad], axis=0).astype(F32)

    def cost(count):
        return pl.CostEstimate(
            flops=count * 12 * w * c * c, bytes_accessed=4 * count * w * c,
            transcendentals=count * w * c)

    bias2 = bias.reshape(1, c)
    small = (u, lh.astype(F32), rh.astype(F32), bias2)
    inner = pl.pallas_call(
        inner_kernel,
        grid=(th // n - 2,),
        out_shape=jax.ShapeDtypeStruct(image.shape, BF16),
        in_specs=[
            one_row(lambda i: (i + 1) * n - 1),
            pl.BlockSpec((n, w, c), lambda i: (i + 1, 0, 0)),
            one_row(lambda i: (i + 2) * n),
            *[whole(x) for x in small],
        ],
        out_specs=pl.BlockSpec((n, w, c), lambda i: (i + 1, 0, 0)),
        compiler_params=params,
        cost_estimate=cost(th - 2 * n),
        name="inner",
    )(image, image, image, *small)

    small = (top, bot, u, column(lh, w), column(rh, w + 1), bias2)
    edges = pl.pallas_call(
        edge_kernel,
        grid=(2,),
        out_shape=jax.ShapeDtypeStruct((2 * n, w, c), BF16),
        in_specs=[
            pl.BlockSpec((n, w, c), lambda i: (i * (th // n - 1), 0, 0)),
            one_row(lambda i: n + i * (th - 2 * n - 1)),
            *[whole(x) for x in small],
        ],
        out_specs=pl.BlockSpec((n, w, c), lambda i: (i, 0, 0)),
        scratch_shapes=[pltpu.VMEM((2, w, c), BF16)],
        compiler_params=params,
        cost_estimate=cost(2 * n),
        name="edges",
    )(image, image, *small)
    out = lax.dynamic_update_slice(inner, edges[:n], (0, 0, 0))
    return lax.dynamic_update_slice(out, edges[n:], (th - n, 0, 0))


def solution(mesh):
    in_specs = (P("row", "col", None), P(), P(), P(), P(), P())
    out_specs = P("row", "col", None)
    return jax.shard_map(
        on_device, mesh=mesh, in_specs=in_specs, out_specs=out_specs, check_vma=False
    )
```

```python
import jax
import jax.numpy as jnp
from jax import lax
from jax.experimental import pallas as pl
from jax.experimental.pallas import tpu as pltpu
from jax.sharding import PartitionSpec as P

BF16 = jnp.bfloat16
F32 = jnp.float32
MIB = 1 << 20
ROWS = 8


def with_sides(x, lead, tail):
    w = x.shape[0]
    left, right = pltpu.roll(x, 1, 0), pltpu.roll(x, w - 1, 0)
    at = lax.broadcasted_iota(jnp.int32, (16, x.shape[1]), 0)
    head = jnp.where(at == 0, lead, left[:16].astype(F32)).astype(BF16)
    foot = jnp.where(at == 15, tail, right[w - 16 :].astype(F32)).astype(BF16)
    left = jnp.concatenate([head, left[16:]], axis=0)
    right = jnp.concatenate([right[: w - 16], foot], axis=0)
    return jnp.concatenate([left, x, right], axis=1)


def conv_kernel(before, here, after, top, bot, u_ref, lh_ref, rh_ref, bias_ref, out_ref,
                ends):
    i = pl.program_id(0)
    n, w, _ = here.shape
    bias = bias_ref[...] * 0.5

    def centre(r):
        return here[r - 1] if 0 < r <= n else ends[r // n]

    def product(k, a, b, add):
        def both(x, y):
            return x + y if add else x - y

        lead, tail = [
            both(ref[pl.ds(i * n + a, 1), :], ref[pl.ds(i * n + b, 1), :]) for ref in (lh_ref, rh_ref)
        ]
        lhs = with_sides(both(centre(a), centre(b)), lead, tail)
        return jnp.dot(lhs, u_ref[k], preferred_element_type=F32)

    def finish(r, half):
        x = here[r].astype(F32)
        out_ref[r] = (x + (half + half * jnp.tanh(half))).astype(BF16)

    ends[0] = jnp.where(i == 0, top[...], before[0])
    ends[1] = jnp.where(i == pl.num_programs(0) - 1, bot[...], after[0])
    for r in range(0, n, 2):
        m1 = product(1, r + 1, r + 2, True)
        m2 = product(2, r + 2, r + 1, False)
        m0 = product(0, r, r + 2, False)
        m3 = product(3, r + 1, r + 3, False)
        finish(r, m0 + (m1 + m2) + bias)
        finish(r + 1, (m1 - m2) - m3 + bias)


def rows_kernel(first, last, rows_ref):
    rows_ref[0] = first[0]
    rows_ref[1] = last[0]


def columns_kernel(left, right, cols_ref):
    for r in range(left.shape[0]):
        cols_ref[0, r : r + 1, :] = left[r].astype(F32)[:1]
        cols_ref[1, r : r + 1, :] = right[r].astype(F32)[-1:]


def weights_kernel(pin_ref, tw_ref, tt_ref, po_ref, u_ref, scaled):
    pin = pin_ref[...].astype(F32)
    c = pin.shape[0]
    t0, t1, t2 = tt_ref[0:1, :], tt_ref[1:2, :], tt_ref[2:3, :]
    mid = 0.5 * (t0 + t2)
    for k, tall in enumerate((t0, mid + 0.5 * t1, mid - 0.5 * t1, t2)):
        for j in range(3):
            scaled[3 * k + j] = (pin * (tall * tw_ref[j : j + 1, :] * 0.5)).astype(BF16)
    for k in range(4):
        for j in range(3):
            u = jnp.dot(scaled[3 * k + j], po_ref[...], preferred_element_type=F32)
            u_ref[k, j * c : (j + 1) * c, :] = u.astype(BF16)


def shifted(x, axis, step):
    count = lax.axis_size(axis)
    if step > 0:
        return lax.ppermute(x, axis, [(i, i + 1) for i in range(count - 1)])
    return lax.ppermute(x, axis, [(i + 1, i) for i in range(count - 1)])


def row_halos(first, last):
    count = lax.axis_size("row")
    if count % 2:
        return shifted(last, "row", 1), shifted(first, "row", -1)
    even = lax.axis_index("row") % 2 == 0

    def swap(x, start):
        pairs = [(i, i + 1) for i in range(start, count - 1, 2)]
        return lax.ppermute(x, "row", pairs + [(b, a) for a, b in pairs])

    got = swap(jnp.where(even, last, first), 0)
    far = swap(jnp.where(even, first, last), 1)
    return jnp.where(even, far, got), jnp.where(even, got, far)


def column_halos(first, last):
    if lax.axis_size("col") == 2:
        low = lax.axis_index("col") == 0
        got = lax.ppermute(jnp.where(low, last, first), "col", [(0, 1), (1, 0)])
        zero = jnp.zeros_like(got)
        return jnp.where(low, zero, got), jnp.where(low, got, zero)
    return shifted(last, "col", 1), shifted(first, "col", -1)


def on_device(image, proj_in, taps_wide, taps_tall, proj_out, bias):
    th, w, c = image.shape
    n = ROWS

    def whole(x):
        return pl.BlockSpec(x.shape, lambda i: (0,) * len(x.shape))

    def one_row(index):
        return pl.BlockSpec((1, w, c), lambda i: (index(i), 0, 0))

    def some_columns(at):
        return pl.BlockSpec((th, 16, c), lambda i: (0, at, 0))

    params = pltpu.CompilerParams(vmem_limit_bytes=48 * MIB)
    rows = jax.ShapeDtypeStruct((2, w, c), BF16)
    rows = pl.pallas_call(
        rows_kernel,
        grid=(1,),
        out_shape=rows,
        in_specs=[one_row(lambda i: 0), one_row(lambda i: th - 1)],
        out_specs=whole(rows),
        compiler_params=params,
        name="rows",
    )(image, image)
    top, bot = row_halos(rows[0], rows[1])

    cols = jax.ShapeDtypeStruct((2, th, c), F32)
    cols = pl.pallas_call(
        columns_kernel,
        grid=(1,),
        out_shape=cols,
        in_specs=[some_columns(0), some_columns(w // 16 - 1)],
        out_specs=whole(cols),
        compiler_params=params,
        cost_estimate=pl.CostEstimate(flops=0, bytes_accessed=3 * MIB, transcendentals=0),
        name="columns",
    )(image, image)

    args = (proj_in, taps_wide, taps_tall, proj_out)
    weights = jax.ShapeDtypeStruct((4, 3 * c, c), BF16)
    u = pl.pallas_call(
        weights_kernel,
        grid=(1,),
        out_shape=weights,
        in_specs=[whole(x) for x in args],
        out_specs=whole(weights),
        scratch_shapes=[pltpu.VMEM((12,) + proj_in.shape, BF16)],
        compiler_params=params,
        cost_estimate=pl.CostEstimate(
            flops=24 * c * c * proj_in.shape[1], bytes_accessed=3 * MIB, transcendentals=0),
        name="weights",
    )(*args)

    def column(k, at):
        pad = jnp.zeros((14, c), BF16)
        return jnp.concatenate(
            [top[at][None], cols[k].astype(BF16), bot[at][None], pad], axis=0)

    lh, rh = column_halos(column(0, 0), column(1, w - 1))
    small = (top, bot, u, lh.astype(F32), rh.astype(F32), bias.reshape(1, c))
    block = pl.BlockSpec((n, w, c), lambda i: (i, 0, 0))
    return pl.pallas_call(
        conv_kernel,
        grid=(th // n,),
        out_shape=jax.ShapeDtypeStruct(image.shape, BF16),
        in_specs=[
            one_row(lambda i: jnp.maximum(i * n - 1, 0)),
            block,
            one_row(lambda i: jnp.minimum(i * n + n, th - 1)),
            *[whole(x) for x in small],
        ],
        out_specs=block,
        scratch_shapes=[pltpu.VMEM((2, w, c), BF16)],
        compiler_params=params,
        name="conv",
    )(image, image, image, *small)


def solution(mesh):
    in_specs = (P("row", "col", None), P(), P(), P(), P(), P())
    out_specs = P("row", "col", None)
    return jax.shard_map(
        on_device, mesh=mesh, in_specs=in_specs, out_specs=out_specs, check_vma=False
    )
```

```python
import jax
import jax.numpy as jnp
from jax import lax
from jax.experimental import pallas as pl
from jax.experimental.pallas import tpu as pltpu
from jax.sharding import PartitionSpec as P

BF16 = jnp.bfloat16
F32 = jnp.float32
MIB = 1 << 20
ROWS = 12


def with_sides(x, lead, tail):
    w = x.shape[0]
    left, right = pltpu.roll(x, 1, 0), pltpu.roll(x, w - 1, 0)
    at = lax.broadcasted_iota(jnp.int32, (16, x.shape[1]), 0)
    head = jnp.where(at == 0, lead, left[:16].astype(F32)).astype(BF16)
    foot = jnp.where(at == 15, tail, right[w - 16 :].astype(F32)).astype(BF16)
    left = jnp.concatenate([head, left[16:]], axis=0)
    right = jnp.concatenate([right[: w - 16], foot], axis=0)
    return jnp.concatenate([left, x, right], axis=1)


def conv_kernel(before, here, after, top, bot, u_ref, lh_ref, rh_ref, bias_ref, out_ref,
                ends):
    i = pl.program_id(0)
    n, w, _ = here.shape
    bias = bias_ref[...] * 0.5

    def centre(r):
        return here[r - 1] if 0 < r <= n else ends[r // n]

    def product(k, a, b, add):
        def both(x, y):
            return x + y if add else x - y

        lead, tail = [
            both(ref[pl.ds(i * n + a, 1), :], ref[pl.ds(i * n + b, 1), :]) for ref in (lh_ref, rh_ref)
        ]
        lhs = with_sides(both(centre(a), centre(b)), lead, tail)
        return jnp.dot(lhs, u_ref[k], preferred_element_type=F32)

    def finish(r, half):
        x = here[r].astype(F32)
        out_ref[r] = (x + (half + half * jnp.tanh(half))).astype(BF16)

    ends[0] = jnp.where(i == 0, top[...], before[0])
    ends[1] = jnp.where(i == pl.num_programs(0) - 1, bot[...], after[0])
    for r in range(0, n, 2):
        m1 = product(1, r + 1, r + 2, True) + bias
        m2 = product(2, r + 2, r + 1, False)
        m0 = product(0, r, r + 2, False)
        m3 = product(3, r + 1, r + 3, False)
        finish(r, m0 + (m1 + m2))
        finish(r + 1, (m1 - m2) - m3)


def rows_kernel(first, last, rows_ref):
    rows_ref[0] = first[0]
    rows_ref[1] = last[0]


def columns_kernel(left, right, cols_ref):
    for r in range(left.shape[0]):
        cols_ref[0, r : r + 1, :] = left[r].astype(F32)[:1]
        cols_ref[1, r : r + 1, :] = right[r].astype(F32)[-1:]


def weights_kernel(pin_ref, tw_ref, tt_ref, po_ref, u_ref, scaled):
    pin = pin_ref[...].astype(F32)
    c = pin.shape[0]
    t0, t1, t2 = tt_ref[0:1, :], tt_ref[1:2, :], tt_ref[2:3, :]
    mid = 0.5 * (t0 + t2)
    for k, tall in enumerate((t0, mid + 0.5 * t1, mid - 0.5 * t1, t2)):
        for j in range(3):
            scaled[3 * k + j] = (pin * (tall * tw_ref[j : j + 1, :] * 0.5)).astype(BF16)
    for k in range(4):
        for j in range(3):
            u = jnp.dot(scaled[3 * k + j], po_ref[...], preferred_element_type=F32)
            u_ref[k, j * c : (j + 1) * c, :] = u.astype(BF16)


def shifted(x, axis, step):
    count = lax.axis_size(axis)
    if step > 0:
        return lax.ppermute(x, axis, [(i, i + 1) for i in range(count - 1)])
    return lax.ppermute(x, axis, [(i + 1, i) for i in range(count - 1)])


def row_halos(first, last):
    count = lax.axis_size("row")
    if count % 2:
        return shifted(last, "row", 1), shifted(first, "row", -1)
    even = lax.axis_index("row") % 2 == 0

    def swap(x, start):
        pairs = [(i, i + 1) for i in range(start, count - 1, 2)]
        return lax.ppermute(x, "row", pairs + [(b, a) for a, b in pairs])

    got = swap(jnp.where(even, last, first), 0)
    far = swap(jnp.where(even, first, last), 1)
    return jnp.where(even, far, got), jnp.where(even, got, far)


def column_halos(first, last):
    if lax.axis_size("col") == 2:
        low = lax.axis_index("col") == 0
        got = lax.ppermute(jnp.where(low, last, first), "col", [(0, 1), (1, 0)])
        zero = jnp.zeros_like(got)
        return jnp.where(low, zero, got), jnp.where(low, got, zero)
    return shifted(last, "col", 1), shifted(first, "col", -1)


def on_device(image, proj_in, taps_wide, taps_tall, proj_out, bias):
    th, w, c = image.shape
    n = ROWS

    def whole(x):
        return pl.BlockSpec(x.shape, lambda i: (0,) * len(x.shape))

    def one_row(index):
        return pl.BlockSpec((1, w, c), lambda i: (index(i), 0, 0))

    def some_columns(at):
        return pl.BlockSpec((th, 16, c), lambda i: (0, at, 0))

    params = pltpu.CompilerParams(vmem_limit_bytes=48 * MIB)
    rows = jax.ShapeDtypeStruct((2, w, c), BF16)
    rows = pl.pallas_call(
        rows_kernel,
        grid=(1,),
        out_shape=rows,
        in_specs=[one_row(lambda i: 0), one_row(lambda i: th - 1)],
        out_specs=whole(rows),
        compiler_params=params,
        name="rows",
    )(image, image)
    top, bot = row_halos(rows[0], rows[1])

    cols = jax.ShapeDtypeStruct((2, th, c), F32)
    cols = pl.pallas_call(
        columns_kernel,
        grid=(1,),
        out_shape=cols,
        in_specs=[some_columns(0), some_columns(w // 16 - 1)],
        out_specs=whole(cols),
        compiler_params=params,
        cost_estimate=pl.CostEstimate(flops=0, bytes_accessed=3 * MIB, transcendentals=0),
        name="columns",
    )(image, image)

    args = (proj_in, taps_wide, taps_tall, proj_out)
    weights = jax.ShapeDtypeStruct((4, 3 * c, c), BF16)
    u = pl.pallas_call(
        weights_kernel,
        grid=(1,),
        out_shape=weights,
        in_specs=[whole(x) for x in args],
        out_specs=whole(weights),
        scratch_shapes=[pltpu.VMEM((12,) + proj_in.shape, BF16)],
        compiler_params=params,
        cost_estimate=pl.CostEstimate(
            flops=24 * c * c * proj_in.shape[1], bytes_accessed=3 * MIB, transcendentals=0),
        name="weights",
    )(*args)

    def column(k, at):
        pad = jnp.zeros((14, c), BF16)
        return jnp.concatenate(
            [top[at][None], cols[k].astype(BF16), bot[at][None], pad], axis=0)

    lh, rh = column_halos(column(0, 0), column(1, w - 1))
    small = (top, bot, u, lh.astype(F32), rh.astype(F32), bias.reshape(1, c))
    block = pl.BlockSpec((n, w, c), lambda i: (i, 0, 0))
    return pl.pallas_call(
        conv_kernel,
        grid=(th // n,),
        out_shape=jax.ShapeDtypeStruct(image.shape, BF16),
        in_specs=[
            one_row(lambda i: jnp.maximum(i * n - 1, 0)),
            block,
            one_row(lambda i: jnp.minimum(i * n + n, th - 1)),
            *[whole(x) for x in small],
        ],
        out_specs=block,
        scratch_shapes=[pltpu.VMEM((2, w, c), BF16)],
        compiler_params=params,
        name="conv",
    )(image, image, image, *small)


def solution(mesh):
    in_specs = (P("row", "col", None), P(), P(), P(), P(), P())
    out_specs = P("row", "col", None)
    return jax.shard_map(
        on_device, mesh=mesh, in_specs=in_specs, out_specs=out_specs, check_vma=False
    )
```
